128 devices in a mesh: dp: 8 (over z, y_hi), tensor: 16 (over x, y_lo, core).
Axes of the slice: x: 4, y: 4 (y_hi: 2, y_lo: 2; y = y_hi * 2 + y_lo), z: 4, core: 2. Of those that a mesh axis runs over, the one named last changes fastest.
Arguments:
- grad: float32 [8192, 8192], P('tensor', 'dp')
- owner_order: int32 [8, 32], P('dp'), may hold values from 0 to 31, each once within a row
- left_stat: float32 [256, 512, 512], P(('dp', 'tensor'))
- right_stat: float32 [256, 512, 512], P(('dp', 'tensor'))
- left_root: bfloat16 [256, 512, 512], P(('dp', 'tensor'))
- right_root: bfloat16 [256, 512, 512], P(('dp', 'tensor'))
- momentum: float32 [256, 512, 512], P(('dp', 'tensor')), may hold values from -6 to 6
- second: float32 [256, 512, 512], P(('dp', 'tensor')), may hold values from 0.25 to 4
Outputs:
- new_left: float32 [256, 512, 512], P(('dp', 'tensor'))
- new_right: float32 [256, 512, 512], P(('dp', 'tensor'))
- new_momentum: float32 [256, 512, 512], P(('dp', 'tensor'))
- new_second: float32 [256, 512, 512], P(('dp', 'tensor'))
- update: float32 [8192, 8192], P('tensor', 'dp')
The draws below stay inside these ranges and needn't reach their ends.
Inputs may be any that keep to these rules, and one draw needn't show every extreme that they name: `owner_order`: each row lists every block number of 0 to 31 once.
All inputs are finite; a program needn't handle non-finite values.
Results may differ from the reference program's by a relative error of at most 0.004.
Values sent between devices are 32-bit elements; how exact they have to be, the bound alone decides.
No kernel may reach another device: no remote copies, remote signals or barrier semaphores. Data moves between devices by JAX's collectives and lax.ppermute only.
A program may use at most 128 MiB of HBM per device.

```python
import math
import jax
import jax.numpy as jnp
from jax import lax

D = 8192
BLOCK = 512
PIECE = 32
ROWG = 16
CPG = 2
COLB = 16
GROUP_BLOCKS = 32
SLOTS = 2
BLOCKS = 256
VOCAB = 8192
N_DP = 8
N_TENSOR = 16


def draw_grad(key, part):
    key = jax.random.fold_in(key, 1)
    first, second_key, third = jax.random.split(key, 3)
    row_rise = jnp.power(3.0, jnp.arange(VOCAB, dtype=jnp.float32) / VOCAB)[:, None]
    row_factor = jnp.exp(jax.random.uniform(second_key, (VOCAB, 1), jnp.float32, 0.0, math.log(3.2)))
    col_factor = jnp.exp(jax.random.uniform(third, (1, D), jnp.float32, 0.0, math.log(3.2)))
    base_draw = jax.random.normal(first, (VOCAB, D), jnp.float32)
    overall = 0.3
    return (overall * base_draw * row_rise * row_factor * col_factor).astype(jnp.float32)


def symmetric_noise(key, spread):
    noise = jax.random.normal(key, (BLOCKS, BLOCK, BLOCK), jnp.float32)
    return spread * 0.5 * (noise + jnp.swapaxes(noise, 1, 2))


def draw_left_stat(key, part):
    key = jax.random.fold_in(key, 2)
    identity_matrix = jnp.eye(BLOCK, dtype=jnp.float32)
    return (symmetric_noise(key, 0.3) + 2.0 * identity_matrix).astype(jnp.float32)


def draw_right_stat(key, part):
    key = jax.random.fold_in(key, 3)
    identity_matrix = jnp.eye(BLOCK, dtype=jnp.float32)
    return (symmetric_noise(key, 0.3) + 2.0 * identity_matrix).astype(jnp.float32)


def root_draw(key):
    noise_key, diag_key = jax.random.split(key)
    identity_matrix = jnp.eye(BLOCK, dtype=jnp.float32)
    diagonal = jnp.exp(jax.random.uniform(diag_key, (BLOCKS, BLOCK, 1), jnp.float32, math.log(0.5), math.log(2.0)))
    return symmetric_noise(noise_key, 0.7 / math.sqrt(BLOCK)) + diagonal * identity_matrix


def draw_left_root(key, part):
    key = jax.random.fold_in(key, 4)
    return root_draw(key).astype(jnp.bfloat16)


def draw_right_root(key, part):
    key = jax.random.fold_in(key, 5)
    return root_draw(key).astype(jnp.bfloat16)


def block_scale(stream_key, extent, cuts, low, top_value):
    def one(dim, parts):
        heights = jax.random.uniform(jax.random.fold_in(jax.random.fold_in(stream_key, 6), dim), (parts,), jnp.float32, low / len(cuts), top_value / len(cuts))
        return jnp.repeat(jnp.exp(heights), extent[dim] // parts).reshape((-1,) + (1,) * (len(extent) - dim - 1))

    loudness = one(*cuts[0])
    for cut in cuts[1:]:
        loudness = loudness * one(*cut)
    return loudness


def centred(own_key, extent, deviation, reach, pieces=(), kind=jnp.bfloat16):
    result = deviation * jax.random.normal(own_key, extent, jnp.float32)
    if pieces:
        result = result * block_scale(own_key, extent, pieces, -0.22, 0.18)
    return jnp.clip(result, -reach, reach).astype(kind)


def setup_inputs(seed: int = 0) -> dict:
    key_of = jax.random.split(jax.random.key(seed), 9)
    grad = draw_grad(jax.random.fold_in(key_of[8], 71), 0)
    owner_order = jax.vmap(lambda own: jax.random.permutation(own, GROUP_BLOCKS))(jax.random.split(key_of[1], N_DP)).reshape((N_DP, GROUP_BLOCKS)).astype(jnp.int32)
    left_stat = draw_left_stat(jax.random.fold_in(key_of[8], 71), 0)
    right_stat = draw_right_stat(jax.random.fold_in(key_of[8], 71), 0)
    left_root = draw_left_root(jax.random.fold_in(key_of[8], 71), 0)
    right_root = draw_right_root(jax.random.fold_in(key_of[8], 71), 0)
    momentum = centred(key_of[6], (BLOCKS, BLOCK, BLOCK), 1.0, 6.0, ((0, 128),), jnp.float32)
    second = jnp.clip(jnp.exp(math.log(4.0) - 2.7725887 * jax.random.uniform(key_of[7], (BLOCKS, BLOCK, BLOCK), jnp.float32) ** block_scale(key_of[7], (BLOCKS, BLOCK, BLOCK), ((0, 128),), -0.2, 0.2)), 0.25, 4.0)
    return {"grad": grad, "owner_order": owner_order, "left_stat": left_stat, "right_stat": right_stat, "left_root": left_root, "right_root": right_root, "momentum": momentum, "second": second}


def slot_blocks(owner_order):
    slot_ids = jnp.arange(BLOCKS, dtype=jnp.int32)
    owner = slot_ids // SLOTS
    local_slot = slot_ids % SLOTS
    dp_index = owner // N_TENSOR
    tp_index = owner % N_TENSOR
    flat_order = owner_order.reshape(-1).astype(jnp.int32)
    block_id = flat_order[dp_index * GROUP_BLOCKS + tp_index * SLOTS + local_slot].astype(jnp.int32)
    row_group = (block_id // CPG).astype(jnp.int32)
    col_block = (dp_index * CPG + block_id % CPG).astype(jnp.int32)
    return (row_group, col_block)

def per_slot(items):
    block_grad, left_old, right_old, left_inv, right_inv = items
    gram_left = jnp.dot(block_grad, block_grad.T, precision=lax.Precision.HIGHEST, preferred_element_type=jnp.float32)
    gram_right = jnp.dot(block_grad.T, block_grad, precision=lax.Precision.HIGHEST, preferred_element_type=jnp.float32)
    left_next = 0.9 * left_old + 0.1 / BLOCK * gram_left
    right_next = 0.9 * right_old + 0.1 / BLOCK * gram_right
    low_grad = block_grad.astype(jnp.bfloat16)
    left_applied = jnp.dot(left_inv, low_grad, preferred_element_type=jnp.float32).astype(jnp.bfloat16)
    shampoo = jnp.dot(left_applied, right_inv, preferred_element_type=jnp.float32)
    return (left_next, right_next, shampoo)

def reference(grad, owner_order, left_stat, right_stat, left_root, right_root, momentum, second):
    row_group, col_block = slot_blocks(owner_order)
    tile_view = grad.reshape(N_TENSOR, ROWG, PIECE, COLB, BLOCK).transpose(1, 3, 0, 2, 4).reshape(ROWG, COLB, BLOCK, BLOCK)
    held = tile_view[row_group, col_block]
    new_left, new_right, shampoo = lax.map(per_slot, (held, left_stat, right_stat, left_root, right_root))
    new_second = 0.99 * second + 0.01 * held * held
    adam = held / (jnp.sqrt(new_second) + 1e-08)
    adam_sq = jnp.sum(adam * adam)
    shampoo_sq = jnp.sum(shampoo * shampoo)
    graft_scale = jnp.sqrt(adam_sq) / (jnp.sqrt(shampoo_sq) + 1e-06)
    new_momentum = 0.9 * momentum + graft_scale * shampoo
    step_blocks = -(0.9 * new_momentum + graft_scale * shampoo)
    placed = jnp.zeros((ROWG, COLB, BLOCK, BLOCK), jnp.float32).at[row_group, col_block].set(step_blocks)
    update = placed.reshape(ROWG, COLB, N_TENSOR, PIECE, BLOCK).transpose(2, 0, 3, 1, 4).reshape(VOCAB, D)
    return (new_left, new_right, new_momentum, new_second, update)
```

```python
import functools

import jax
import jax.numpy as jnp
from jax import lax
from jax.experimental import pallas as pl
from jax.experimental.pallas import tpu as pltpu
from jax.sharding import PartitionSpec as P

ANY = pl.BlockSpec(memory_space=pl.ANY)
VMEM = pl.BlockSpec(memory_space=pltpu.VMEM)
DMA = pltpu.SemaphoreType.DMA
MIB = 1 << 20
F32 = jnp.float32
BF16 = jnp.bfloat16
CHUNKS = 4


def in_vmem(x):
    return pltpu.with_memory_space_constraint(x, pltpu.VMEM)


def in_hbm(x):
    return pltpu.with_memory_space_constraint(x, pltpu.HBM)


def params(mib):
    return pltpu.CompilerParams(vmem_limit_bytes=mib * MIB)


def copy(source, target, sem):
    return pltpu.make_async_copy(source, target, sem)


def started(source, target, sem):
    moved = copy(source, target, sem)
    moved.start()
    return moved


def wait_all(ref, sem):
    copy(ref, ref, sem).wait()


def piece_of(ref, block, piece_rows, block_size):
    col_blocks = ref.shape[1] // block_size
    row = pl.multiple_of((block // col_blocks) * piece_rows, piece_rows)
    col = pl.multiple_of((block % col_blocks) * block_size, block_size)
    return ref.at[pl.ds(row, piece_rows), pl.ds(col, block_size)]


def rows_of(peer, piece_rows):
    return slice(peer * piece_rows, (peer + 1) * piece_rows)


def pack_kernel(order_ref, grad_ref, out_ref, sem):
    peers, slots, piece_rows, block_size = out_ref.shape
    for peer in range(peers):
        for slot in range(slots):
            block = order_ref[0, peer * slots + slot]
            started(
                piece_of(grad_ref, block, piece_rows, block_size), out_ref.at[peer, slot], sem
            )
    wait_all(out_ref, sem)


def unpack_kernel(order_ref, moved_ref, out_ref, sem):
    peers, slots, piece_rows, block_size = moved_ref.shape
    for peer in range(peers):
        for slot in range(slots):
            block = order_ref[0, peer * slots + slot]
            started(
                moved_ref.at[peer, slot], piece_of(out_ref, block, piece_rows, block_size), sem
            )
    wait_all(moved_ref, sem)


def sum_rows(x):
    return jnp.sum(x.reshape(-1, 8, x.shape[-1]), axis=0)


def mid_kernel(
    arrived_ref, second_ref, left_ref, right_ref, shampoo_ref, held_ref, sums_ref, low_ref, sem
):
    peers, slots, piece_rows, block_size = arrived_ref.shape
    half = block_size // 2
    half_peers = peers // 2
    kept = started(arrived_ref, held_ref, sem)
    adam_sq = jnp.zeros((8, block_size), F32)
    shampoo_sq = jnp.zeros((8, block_size), F32)
    for slot in range(slots):
        for peer in range(peers):
            rows = rows_of(peer, piece_rows)
            held = arrived_ref[peer, slot]
            low_ref[slot, rows, :] = held.astype(BF16)
            new_second = 0.99 * second_ref[slot, rows, :] + 0.01 * held * held
            adam = held / (jnp.sqrt(new_second) + 1e-08)
            adam_sq += sum_rows(adam * adam)
    for slot in range(slots):
        for part in range(2):
            rows = slice(part * half, (part + 1) * half)
            left_applied = jnp.dot(
                left_ref[slot, rows, :], low_ref[slot], preferred_element_type=F32
            ).astype(BF16)
            shampoo = jnp.dot(left_applied, right_ref[slot], preferred_element_type=F32)
            shampoo_ref[part * half_peers : (part + 1) * half_peers, slot] = shampoo.reshape(
                half_peers, piece_rows, block_size
            )
            shampoo_sq += sum_rows(shampoo * shampoo)
    ranks = sums_ref.shape[0]
    sums_ref[:, 0, :] = jnp.full((ranks, 128), jnp.sum(adam_sq), F32)
    sums_ref[:, 1, :] = jnp.full((ranks, 128), jnp.sum(shampoo_sq), F32)
    kept.wait()


def graft_of(sums_ref):
    root = jnp.sqrt(jnp.sum(sums_ref[...], axis=0))
    return root[0:1, 0:1] / (root[1:2, 0:1] + 1e-06)


def gram_kernel(
    held_ref, second_ref, left_ref, right_ref,
    new_left_ref, new_right_ref, new_second_ref,
    held_here, second_here, left_here, right_here, high_ref, low_ref, sems, store_sem,
):
    peers, slots, piece_rows, block_size = held_ref.shape
    loads = [
        [
            started(source.at[(*at, slot)], target.at[(*at, slot)], sems.at[slot, k])
            for k, (source, target, at) in enumerate(
                (
                    (held_ref, held_here, (slice(None),)),
                    (left_ref, left_here, ()),
                    (right_ref, right_here, ()),
                    (second_ref, second_here, ()),
                )
            )
        ]
        for slot in range(slots)
    ]
    scale = 0.1 / block_size
    half = block_size // 2
    for slot in range(slots):
        loads[slot][0].wait()
        for peer in range(peers):
            rows = rows_of(peer, piece_rows)
            held = held_here[peer, slot]
            high = held.astype(BF16)
            high_ref[slot, rows, :] = high
            low_ref[slot, rows, :] = (held - high.astype(F32)).astype(BF16)
        for k, (here, ref) in enumerate(
            ((left_here, new_left_ref), (right_here, new_right_ref))
        ):
            product = functools.partial(
                lax.dot_general,
                dimension_numbers=(((1 - k,), (1 - k,)), ((), ())),
                preferred_element_type=F32,
            )
            loads[slot][1 + k].wait()
            for part in range(2):
                cut = slice(part * half, (part + 1) * half)
                at = (slot, cut, slice(None)) if k == 0 else (slot, slice(None), cut)
                gram = (
                    product(high_ref[at], low_ref[slot])
                    + product(low_ref[at], high_ref[slot])
                    + product(high_ref[at], high_ref[slot])
                )
                here[slot, cut, :] = 0.9 * here[slot, cut, :] + scale * gram
            started(here.at[slot], ref.at[slot], store_sem)
        loads[slot][3].wait()
        for peer in range(peers):
            rows = rows_of(peer, piece_rows)
            held = held_here[peer, slot]
            second_here[slot, rows, :] = 0.99 * second_here[slot, rows, :] + 0.01 * held * held
        started(second_here.at[slot], new_second_ref.at[slot], store_sem)
    for here in (left_here, right_here, second_here):
        wait_all(here, store_sem)


def step_kernel(
    sums_ref, shampoo_ref, momentum_ref, _, step_ref, new_momentum_ref, here_ref, sems, store_sem
):
    peers, slots, piece_rows, block_size = shampoo_ref.shape
    count = peers // CHUNKS
    parts = [
        (slot, chunk, (slot, pl.ds(chunk * count * piece_rows, count * piece_rows)))
        for chunk in range(CHUNKS)
        for slot in range(slots)
    ]
    loads = [
        started(momentum_ref.at[at], here_ref.at[at], sems.at[slot, chunk])
        for slot, chunk, at in parts
    ]
    graft = graft_of(sums_ref)
    for load, (slot, chunk, at) in zip(loads, parts):
        load.wait()
        for peer in range(chunk * count, (chunk + 1) * count):
            rows = rows_of(peer, piece_rows)
            scaled = graft * shampoo_ref[peer, slot]
            new_momentum = 0.9 * here_ref[slot, rows, :] + scaled
            here_ref[slot, rows, :] = new_momentum
            step_ref[peer, slot] = -(0.9 * new_momentum + scaled)
        started(here_ref.at[at], new_momentum_ref.at[at], store_sem)
    wait_all(here_ref, store_sem)


def body(grad, owner_order, left_stat, right_stat, left_root, right_root, momentum, second):
    slots, block_size = left_stat.shape[0], left_stat.shape[1]
    peers = lax.axis_size("tensor")
    ranks = peers * lax.axis_size("dp")
    piece_rows = block_size // peers
    pair = (peers, slots, piece_rows, block_size)
    blocks = (slots, block_size, block_size)
    hbm = lambda shape: pltpu.HBM(shape, F32)
    vmem = lambda shape, dtype=F32: pltpu.VMEM(shape, dtype)
    over_tensor = functools.partial(
        lax.all_to_all, axis_name="tensor", split_axis=0, concat_axis=0, tiled=True
    )
    order = in_hbm(owner_order)

    outgoing = pl.pallas_call(
        pack_kernel,
        out_shape=jax.ShapeDtypeStruct(pair, F32),
        grid_spec=pltpu.PrefetchScalarGridSpec(
            num_scalar_prefetch=1, grid=(1,), in_specs=[ANY], out_specs=ANY,
            scratch_shapes=[DMA],
        ),
        compiler_params=params(2),
        name="pack",
    )(order, in_hbm(grad))
    arrived = over_tensor(outgoing)

    shampoo, held, sums = pl.pallas_call(
        mid_kernel,
        out_shape=(vmem(pair), hbm(pair), hbm((ranks, 2, 128))),
        in_specs=[VMEM] * 4,
        out_specs=(VMEM, ANY, VMEM),
        scratch_shapes=[vmem(blocks, BF16), DMA],
        compiler_params=params(16),
        name="mid",
    )(in_vmem(arrived), in_vmem(second), in_vmem(left_root), in_vmem(right_root))
    sums = lax.all_to_all(
        sums, ("dp", "tensor"), split_axis=0, concat_axis=0, tiled=True
    )

    new_left, new_right, new_second = pl.pallas_call(
        gram_kernel,
        out_shape=(hbm(blocks),) * 3,
        in_specs=[ANY] * 4,
        out_specs=(ANY,) * 3,
        scratch_shapes=[vmem(pair)] + [vmem(blocks)] * 3 + [vmem(blocks, BF16)] * 2
        + [DMA((slots, 4)), DMA],
        compiler_params=params(24),
        cost_estimate=pl.CostEstimate(
            flops=slots * 12 * block_size**3, bytes_accessed=14 * MIB, transcendentals=0
        ),
        name="gram",
    )(in_hbm(held), in_hbm(second), in_hbm(left_stat), in_hbm(right_stat))

    step, new_momentum = pl.pallas_call(
        step_kernel,
        out_shape=(vmem(pair), hbm(blocks)),
        in_specs=[VMEM, VMEM, ANY, ANY],
        out_specs=(VMEM, ANY),
        scratch_shapes=[vmem(blocks), DMA((slots, CHUNKS)), DMA],
        compiler_params=params(8),
        name="step",
    )(sums, in_vmem(shampoo), in_hbm(momentum), in_hbm(new_second))
    returned = over_tensor(step)

    update = pl.pallas_call(
        unpack_kernel,
        out_shape=hbm(grad.shape),
        grid_spec=pltpu.PrefetchScalarGridSpec(
            num_scalar_prefetch=1, grid=(1,), in_specs=[ANY], out_specs=ANY,
            scratch_shapes=[DMA],
        ),
        compiler_params=params(2),
        name="unpack",
    )(order, in_vmem(returned))
    return (new_left, new_right, new_momentum, new_second, update)


def solution(mesh):
    owned = P(("dp", "tensor"), None, None)
    return jax.shard_map(
        body,
        mesh=mesh,
        in_specs=(P("tensor", "dp"), P("dp", None)) + (owned,) * 6,
        out_specs=(owned,) * 4 + (P("tensor", "dp"),),
        check_vma=False,
    )
```

```python
import functools

import jax
import jax.numpy as jnp
from jax import lax
from jax.experimental import pallas as pl
from jax.experimental.pallas import tpu as pltpu
from jax.sharding import PartitionSpec as P

ANY = pl.BlockSpec(memory_space=pl.ANY)
VMEM = pl.BlockSpec(memory_space=pltpu.VMEM)
DMA = pltpu.SemaphoreType.DMA
MIB = 1 << 20
F32 = jnp.float32
BF16 = jnp.bfloat16
CHUNKS = 4


def in_vmem(x):
    return pltpu.with_memory_space_constraint(x, pltpu.VMEM)


def in_hbm(x):
    return pltpu.with_memory_space_constraint(x, pltpu.HBM)


def params(mib):
    return pltpu.CompilerParams(vmem_limit_bytes=mib * MIB)


def copy(source, target, sem):
    return pltpu.make_async_copy(source, target, sem)


def started(source, target, sem):
    moved = copy(source, target, sem)
    moved.start()
    return moved


def wait_all(ref, sem):
    copy(ref, ref, sem).wait()


def piece_of(ref, block, piece_rows, block_size):
    col_blocks = ref.shape[1] // block_size
    row = pl.multiple_of((block // col_blocks) * piece_rows, piece_rows)
    col = pl.multiple_of((block % col_blocks) * block_size, block_size)
    return ref.at[pl.ds(row, piece_rows), pl.ds(col, block_size)]


def rows_of(peer, piece_rows):
    return slice(peer * piece_rows, (peer + 1) * piece_rows)


def pack_kernel(order_ref, grad_ref, out_ref, sem):
    peers, slots, piece_rows, block_size = out_ref.shape
    for peer in range(peers):
        for slot in range(slots):
            block = order_ref[0, peer * slots + slot]
            started(
                piece_of(grad_ref, block, piece_rows, block_size), out_ref.at[peer, slot], sem
            )
    wait_all(out_ref, sem)


def unpack_kernel(order_ref, moved_ref, out_ref, sem):
    peers, slots, piece_rows, block_size = moved_ref.shape
    for peer in range(peers):
        for slot in range(slots):
            block = order_ref[0, peer * slots + slot]
            started(
                moved_ref.at[peer, slot], piece_of(out_ref, block, piece_rows, block_size), sem
            )
    wait_all(moved_ref, sem)


def sum_rows(x):
    return jnp.sum(x.reshape(-1, 8, x.shape[-1]), axis=0)


def mid_kernel(
    arrived_ref, second_ref, left_ref, right_ref, shampoo_ref, sums_ref, low_ref, here_ref, sem
):
    peers, slots, piece_rows, block_size = arrived_ref.shape
    half = block_size // 2
    half_peers = peers // 2
    adam_sq = jnp.zeros((8, block_size), F32)
    shampoo_sq = jnp.zeros((8, block_size), F32)
    for slot in range(slots):
        for peer in range(peers):
            low_ref[slot, rows_of(peer, piece_rows), :] = arrived_ref[peer, slot].astype(BF16)
    for slot in range(slots):
        for part in range(2):
            rows = slice(part * half, (part + 1) * half)
            left_applied = jnp.dot(
                left_ref[slot, rows, :], low_ref[slot], preferred_element_type=F32
            ).astype(BF16)
            shampoo = jnp.dot(left_applied, right_ref[slot], preferred_element_type=F32)
            at = (pl.ds(part * half_peers, half_peers), slot)
            here_ref[at] = shampoo.reshape(half_peers, piece_rows, block_size)
            started(here_ref.at[at], shampoo_ref.at[at], sem)
            shampoo_sq += sum_rows(shampoo * shampoo)
    for slot in range(slots):
        for peer in range(peers):
            held = arrived_ref[peer, slot]
            new_second = (
                0.99 * second_ref[slot, rows_of(peer, piece_rows), :] + 0.01 * held * held
            )
            adam = held / (jnp.sqrt(new_second) + 1e-08)
            adam_sq += sum_rows(adam * adam)
    ranks = sums_ref.shape[0]
    sums_ref[:, 0, :] = jnp.full((ranks, 128), jnp.sum(adam_sq), F32)
    sums_ref[:, 1, :] = jnp.full((ranks, 128), jnp.sum(shampoo_sq), F32)
    wait_all(here_ref, sem)


def graft_of(sums_ref):
    root = jnp.sqrt(jnp.sum(sums_ref[...], axis=0))
    return root[0:1, 0:1] / (root[1:2, 0:1] + 1e-06)


def gram_kernel(
    arrived_ref, second_ref, left_ref, right_ref,
    new_left_ref, new_right_ref, new_second_ref,
    second_here, left_here, right_here, low_ref, sems, store_sem,
):
    peers, slots, piece_rows, block_size = arrived_ref.shape
    loads = [
        [
            started(source.at[slot], target.at[slot], sems.at[slot, k])
            for k, (source, target) in enumerate(
                ((left_ref, left_here), (right_ref, right_here), (second_ref, second_here))
            )
        ]
        for slot in range(slots)
    ]
    scale = 0.1 / block_size
    half = block_size // 2
    for slot in range(slots):
        for peer in range(peers):
            low_ref[slot, rows_of(peer, piece_rows), :] = arrived_ref[peer, slot].astype(BF16)
    for slot in range(slots):
        for k, (here, ref) in enumerate(
            ((left_here, new_left_ref), (right_here, new_right_ref))
        ):
            loads[slot][k].wait()
            for part in range(2):
                cut = slice(part * half, (part + 1) * half)
                at = (slot, cut, slice(None)) if k == 0 else (slot, slice(None), cut)
                gram = lax.dot_general(
                    low_ref[at], low_ref[slot], (((1 - k,), (1 - k,)), ((), ())),
                    preferred_element_type=F32,
                )
                here[slot, cut, :] = 0.9 * here[slot, cut, :] + scale * gram
            started(here.at[slot], ref.at[slot], store_sem)
        loads[slot][2].wait()
        for peer in range(peers):
            rows = rows_of(peer, piece_rows)
            held = arrived_ref[peer, slot]
            second_here[slot, rows, :] = 0.99 * second_here[slot, rows, :] + 0.01 * held * held
        started(second_here.at[slot], new_second_ref.at[slot], store_sem)
    for here in (left_here, right_here, second_here):
        wait_all(here, store_sem)


def step_kernel(
    sums_ref, shampoo_ref, momentum_ref, _, step_ref, new_momentum_ref, here_ref, sems, store_sem
):
    peers, slots, piece_rows, block_size = shampoo_ref.shape
    count = peers // CHUNKS
    parts = [
        (slot, chunk, (slot, pl.ds(chunk * count * piece_rows, count * piece_rows)))
        for chunk in range(CHUNKS)
        for slot in range(slots)
    ]
    loads = [
        started(momentum_ref.at[at], here_ref.at[at], sems.at[slot, chunk])
        for slot, chunk, at in parts
    ]
    graft = graft_of(sums_ref)
    for load, (slot, chunk, at) in zip(loads, parts):
        load.wait()
        for peer in range(chunk * count, (chunk + 1) * count):
            rows = rows_of(peer, piece_rows)
            scaled = graft * shampoo_ref[peer, slot]
            new_momentum = 0.9 * here_ref[slot, rows, :] + scaled
            here_ref[slot, rows, :] = new_momentum
            step_ref[peer, slot] = -(0.9 * new_momentum + scaled)
        started(here_ref.at[at], new_momentum_ref.at[at], store_sem)
    wait_all(here_ref, store_sem)


def body(grad, owner_order, left_stat, right_stat, left_root, right_root, momentum, second):
    slots, block_size = left_stat.shape[0], left_stat.shape[1]
    peers = lax.axis_size("tensor")
    ranks = peers * lax.axis_size("dp")
    piece_rows = block_size // peers
    pair = (peers, slots, piece_rows, block_size)
    blocks = (slots, block_size, block_size)
    hbm = lambda shape: pltpu.HBM(shape, F32)
    vmem = lambda shape, dtype=F32: pltpu.VMEM(shape, dtype)
    over_tensor = functools.partial(
        lax.all_to_all, axis_name="tensor", split_axis=0, concat_axis=0, tiled=True
    )
    order = in_hbm(owner_order)

    outgoing = pl.pallas_call(
        pack_kernel,
        out_shape=jax.ShapeDtypeStruct(pair, F32),
        grid_spec=pltpu.PrefetchScalarGridSpec(
            num_scalar_prefetch=1, grid=(1,), in_specs=[ANY], out_specs=ANY,
            scratch_shapes=[DMA],
        ),
        compiler_params=params(2),
        name="pack",
    )(order, in_hbm(grad))
    arrived = in_vmem(over_tensor(outgoing))

    shampoo, sums = pl.pallas_call(
        mid_kernel,
        out_shape=(hbm(pair), hbm((ranks, 2, 128))),
        in_specs=[VMEM] * 4,
        out_specs=(ANY, VMEM),
        scratch_shapes=[vmem(blocks, BF16), vmem(pair), DMA],
        compiler_params=params(16),
        name="mid",
    )(arrived, in_vmem(second), in_vmem(left_root), in_vmem(right_root))
    sums = lax.all_to_all(
        sums, ("dp", "tensor"), split_axis=0, concat_axis=0, tiled=True
    )

    new_left, new_right, new_second = pl.pallas_call(
        gram_kernel,
        out_shape=(hbm(blocks),) * 3,
        in_specs=[VMEM] + [ANY] * 3,
        out_specs=(ANY,) * 3,
        scratch_shapes=[vmem(blocks)] * 3 + [vmem(blocks, BF16), DMA((slots, 3)), DMA],
        compiler_params=params(16),
        cost_estimate=pl.CostEstimate(
            flops=slots * 12 * block_size**3, bytes_accessed=14 * MIB, transcendentals=0
        ),
        name="gram",
    )(arrived, in_hbm(second), in_hbm(left_stat), in_hbm(right_stat))

    step, new_momentum = pl.pallas_call(
        step_kernel,
        out_shape=(vmem(pair), hbm(blocks)),
        in_specs=[VMEM, VMEM, ANY, ANY],
        out_specs=(VMEM, ANY),
        scratch_shapes=[vmem(blocks), DMA((slots, CHUNKS)), DMA],
        compiler_params=params(8),
        name="step",
    )(sums, in_vmem(shampoo), in_hbm(momentum), in_hbm(new_second))
    returned = over_tensor(step)

    update = pl.pallas_call(
        unpack_kernel,
        out_shape=hbm(grad.shape),
        grid_spec=pltpu.PrefetchScalarGridSpec(
            num_scalar_prefetch=1, grid=(1,), in_specs=[ANY], out_specs=ANY,
            scratch_shapes=[DMA],
        ),
        compiler_params=params(2),
        name="unpack",
    )(order, in_vmem(returned))
    return (new_left, new_right, new_momentum, new_second, update)


def solution(mesh):
    owned = P(("dp", "tensor"), None, None)
    return jax.shard_map(
        body,
        mesh=mesh,
        in_specs=(P("tensor", "dp"), P("dp", None)) + (owned,) * 6,
        out_specs=(owned,) * 4 + (P("tensor", "dp"),),
        check_vma=False,
    )
```

```python
import functools

import jax
import jax.numpy as jnp
from jax import lax
from jax.experimental import pallas as pl
from jax.experimental.pallas import tpu as pltpu
from jax.sharding import PartitionSpec as P

ANY = pl.BlockSpec(memory_space=pl.ANY)
VMEM = pl.BlockSpec(memory_space=pltpu.VMEM)
DMA = pltpu.SemaphoreType.DMA
MIB = 1 << 20
F32 = jnp.float32
BF16 = jnp.bfloat16
CHUNKS = 4


def in_vmem(x):
    return pltpu.with_memory_space_constraint(x, pltpu.VMEM)


def in_hbm(x):
    return pltpu.with_memory_space_constraint(x, pltpu.HBM)


def params(mib):
    return pltpu.CompilerParams(vmem_limit_bytes=mib * MIB)


def copy(source, target, sem):
    return pltpu.make_async_copy(source, target, sem)


def started(source, target, sem):
    moved = copy(source, target, sem)
    moved.start()
    return moved


def wait_all(ref, sem):
    copy(ref, ref, sem).wait()


def piece_of(ref, block, piece_rows, block_size):
    col_blocks = ref.shape[1] // block_size
    row = pl.multiple_of((block // col_blocks) * piece_rows, piece_rows)
    col = pl.multiple_of((block % col_blocks) * block_size, block_size)
    return ref.at[pl.ds(row, piece_rows), pl.ds(col, block_size)]


def rows_of(peer, piece_rows):
    return slice(peer * piece_rows, (peer + 1) * piece_rows)


def pack_kernel(order_ref, grad_ref, out_ref, sem):
    peers, slots, piece_rows, block_size = out_ref.shape
    for peer in range(peers):
        for slot in range(slots):
            block = order_ref[0, peer * slots + slot]
            started(
                piece_of(grad_ref, block, piece_rows, block_size), out_ref.at[peer, slot], sem
            )
    wait_all(out_ref, sem)


def unpack_kernel(order_ref, moved_ref, out_ref, sem):
    peers, slots, piece_rows, block_size = moved_ref.shape
    for peer in range(peers):
        for slot in range(slots):
            block = order_ref[0, peer * slots + slot]
            started(
                moved_ref.at[peer, slot], piece_of(out_ref, block, piece_rows, block_size), sem
            )
    wait_all(moved_ref, sem)


def sum_rows(x):
    return jnp.sum(x.reshape(-1, 8, x.shape[-1]), axis=0)


def mid_kernel(
    arrived_ref, second_ref, left_ref, right_ref, shampoo_ref, held_ref, sums_ref, low_ref, sem
):
    peers, slots, piece_rows, block_size = arrived_ref.shape
    half = block_size // 2
    half_peers = peers // 2
    kept = started(arrived_ref, held_ref, sem)
    adam_sq = jnp.zeros((8, block_size), F32)
    shampoo_sq = jnp.zeros((8, block_size), F32)
    for slot in range(slots):
        for peer in range(peers):
            rows = rows_of(peer, piece_rows)
            held = arrived_ref[peer, slot]
            low_ref[slot, rows, :] = held.astype(BF16)
            new_second = 0.99 * second_ref[slot, rows, :] + 0.01 * held * held
            adam = held / (jnp.sqrt(new_second) + 1e-08)
            adam_sq += sum_rows(adam * adam)
    for slot in range(slots):
        for part in range(2):
            rows = slice(part * half, (part + 1) * half)
            left_applied = jnp.dot(
                left_ref[slot, rows, :], low_ref[slot], preferred_element_type=F32
            ).astype(BF16)
            shampoo = jnp.dot(left_applied, right_ref[slot], preferred_element_type=F32)
            shampoo_ref[part * half_peers : (part + 1) * half_peers, slot] = shampoo.reshape(
                half_peers, piece_rows, block_size
            )
            shampoo_sq += sum_rows(shampoo * shampoo)
    ranks = sums_ref.shape[0]
    sums_ref[:, 0, :] = jnp.full((ranks, 128), jnp.sum(adam_sq), F32)
    sums_ref[:, 1, :] = jnp.full((ranks, 128), jnp.sum(shampoo_sq), F32)
    kept.wait()


def graft_of(sums_ref):
    root = jnp.sqrt(jnp.sum(sums_ref[...], axis=0))
    return root[0:1, 0:1] / (root[1:2, 0:1] + 1e-06)


def step_kernel(sums_ref, shampoo_ref, momentum_ref, step_ref, here_ref, sem):
    peers, slots, piece_rows, block_size = shampoo_ref.shape
    graft = graft_of(sums_ref)
    count = peers // CHUNKS
    for peer in range(peers):
        rows = rows_of(peer, piece_rows)
        for slot in range(slots):
            scaled = graft * shampoo_ref[peer, slot]
            new_momentum = 0.9 * momentum_ref[slot, rows, :] + scaled
            here_ref[peer, slot] = -(0.9 * new_momentum + scaled)
        if peer % count == count - 1:
            part = pl.ds(peer - count + 1, count)
            started(here_ref.at[part], step_ref.at[part], sem)
    wait_all(here_ref, sem)


def rest_kernel(
    held_ref, second_ref, left_ref, right_ref, momentum_ref, step_ref,
    new_left_ref, new_right_ref, new_second_ref, new_momentum_ref,
    held_here, second_here, left_here, right_here, momentum_here, step_here, high_ref, low_ref,
    sems, store_sem,
):
    peers, slots, piece_rows, block_size = held_ref.shape
    loads = []
    for slot in range(slots):
        pairs = (
            (left_ref.at[slot], left_here.at[slot]),
            (right_ref.at[slot], right_here.at[slot]),
            (second_ref.at[slot], second_here.at[slot]),
            (momentum_ref.at[slot], momentum_here.at[slot]),
            (step_ref.at[:, slot], step_here.at[:, slot]),
            (held_ref.at[:, slot], held_here.at[:, slot]),
        )[::-1]
        loads.append([started(*pair, sems.at[slot, k]) for k, pair in enumerate(pairs)])
    scale = 0.1 / block_size
    half = block_size // 2
    for slot in range(slots):
        loads[slot][0].wait()
        for peer in range(peers):
            rows = rows_of(peer, piece_rows)
            held = held_here[peer, slot]
            high = held.astype(BF16)
            high_ref[slot, rows, :] = high
            low_ref[slot, rows, :] = (held - high.astype(F32)).astype(BF16)
        for k, (here, ref) in enumerate(
            ((left_here, new_left_ref), (right_here, new_right_ref))
        ):
            product = functools.partial(
                lax.dot_general,
                dimension_numbers=(((1 - k,), (1 - k,)), ((), ())),
                preferred_element_type=F32,
            )
            loads[slot][5 - k].wait()
            for part in range(2):
                cut = slice(part * half, (part + 1) * half)
                at = (slot, cut, slice(None)) if k == 0 else (slot, slice(None), cut)
                gram = (
                    product(high_ref[at], low_ref[slot])
                    + product(low_ref[at], high_ref[slot])
                    + product(high_ref[at], high_ref[slot])
                )
                here[slot, cut, :] = 0.9 * here[slot, cut, :] + scale * gram
            started(here.at[slot], ref.at[slot], store_sem)
        for load in loads[slot][1:4]:
            load.wait()
        for peer in range(peers):
            rows = rows_of(peer, piece_rows)
            held = held_here[peer, slot]
            second_here[slot, rows, :] = 0.99 * second_here[slot, rows, :] + 0.01 * held * held
            momentum_here[slot, rows, :] = (
                0.9 * momentum_here[slot, rows, :] - step_here[peer, slot]
            ) * (1.0 / 1.9)
        started(second_here.at[slot], new_second_ref.at[slot], store_sem)
        started(momentum_here.at[slot], new_momentum_ref.at[slot], store_sem)
    for here in (left_here, right_here, second_here, momentum_here):
        wait_all(here, store_sem)


def body(grad, owner_order, left_stat, right_stat, left_root, right_root, momentum, second):
    slots, block_size = left_stat.shape[0], left_stat.shape[1]
    peers = lax.axis_size("tensor")
    ranks = peers * lax.axis_size("dp")
    piece_rows = block_size // peers
    pair = (peers, slots, piece_rows, block_size)
    blocks = (slots, block_size, block_size)
    hbm = lambda shape: pltpu.HBM(shape, F32)
    vmem = lambda shape, dtype=F32: pltpu.VMEM(shape, dtype)
    over_tensor = functools.partial(
        lax.all_to_all, axis_name="tensor", split_axis=0, concat_axis=0, tiled=True
    )
    order = in_hbm(owner_order)

    outgoing = pl.pallas_call(
        pack_kernel,
        out_shape=jax.ShapeDtypeStruct(pair, F32),
        grid_spec=pltpu.PrefetchScalarGridSpec(
            num_scalar_prefetch=1, grid=(1,), in_specs=[ANY], out_specs=ANY,
            scratch_shapes=[DMA],
        ),
        compiler_params=params(2),
        name="pack",
    )(order, in_hbm(grad))
    arrived = over_tensor(outgoing)

    shampoo, held, sums = pl.pallas_call(
        mid_kernel,
        out_shape=(vmem(pair), hbm(pair), jax.ShapeDtypeStruct((ranks, 2, 128), F32)),
        in_specs=[VMEM] * 4,
        out_specs=(VMEM, ANY, VMEM),
        scratch_shapes=[vmem(blocks, BF16), DMA],
        compiler_params=params(16),
        name="mid",
    )(in_vmem(arrived), in_vmem(second), in_vmem(left_root), in_vmem(right_root))
    sums = lax.all_to_all(
        sums, ("dp", "tensor"), split_axis=0, concat_axis=0, tiled=True
    )

    step = pl.pallas_call(
        step_kernel,
        out_shape=hbm(pair),
        in_specs=[VMEM] * 3,
        out_specs=ANY,
        scratch_shapes=[vmem(pair), DMA],
        compiler_params=params(8),
        name="step",
    )(sums, in_vmem(shampoo), in_vmem(momentum))
    returned = over_tensor(step)

    new_left, new_right, new_second, new_momentum = pl.pallas_call(
        rest_kernel,
        out_shape=(hbm(blocks),) * 4,
        in_specs=[ANY] * 6,
        out_specs=(ANY,) * 4,
        scratch_shapes=[vmem(pair)] + [vmem(blocks)] * 4 + [vmem(pair)]
        + [vmem(blocks, BF16)] * 2 + [DMA((slots, 6)), DMA],
        compiler_params=params(24),
        cost_estimate=pl.CostEstimate(
            flops=slots * 12 * block_size**3, bytes_accessed=18 * MIB, transcendentals=0
        ),
        name="rest",
    )(
        in_hbm(held), in_hbm(second), in_hbm(left_stat), in_hbm(right_stat),
        in_hbm(momentum), in_hbm(step),
    )

    update = pl.pallas_call(
        unpack_kernel,
        out_shape=hbm(grad.shape),
        in_specs=[pl.BlockSpec(memory_space=pltpu.SMEM), VMEM],
        out_specs=ANY,
        scratch_shapes=[DMA],
        compiler_params=params(8),
        name="unpack",
    )(order, in_vmem(returned))
    return (new_left, new_right, new_momentum, new_second, update)


def solution(mesh):
    owned = P(("dp", "tensor"), None, None)
    return jax.shard_map(
        body,
        mesh=mesh,
        in_specs=(P("tensor", "dp"), P("dp", None)) + (owned,) * 6,
        out_specs=(owned,) * 4 + (P("tensor", "dp"),),
        check_vma=False,
    )
```

```python
import functools

import jax
import jax.numpy as jnp
import numpy as np
from jax import lax
from jax.experimental import pallas as pl
from jax.experimental.pallas import tpu as pltpu
from jax.sharding import PartitionSpec as P

ANY = pl.BlockSpec(memory_space=pl.ANY)
VMEM = pl.BlockSpec(memory_space=pltpu.VMEM)
DMA = pltpu.SemaphoreType.DMA
MIB = 1 << 20
F32 = jnp.float32
BF16 = jnp.bfloat16
CHUNKS = 4


FINE = (("z", 4), ("yh", 2), ("x", 4), ("yl", 2), ("core", 2))
DP, TENSOR = ("z", "yh"), ("x", "yl", "core")
OUT_ORDER, BACK_ORDER = TENSOR, TENSOR


def places_of(order):
    sizes = dict(FINE)
    places = []
    for at in np.ndindex(*(sizes[axis] for axis in order)):
        where = dict(zip(order, at))
        place = 0
        for axis in TENSOR:
            place = place * sizes[axis] + where[axis]
        places.append(place)
    return places


def in_vmem(x):
    return pltpu.with_memory_space_constraint(x, pltpu.VMEM)


def in_hbm(x):
    return pltpu.with_memory_space_constraint(x, pltpu.HBM)


def params(mib):
    return pltpu.CompilerParams(vmem_limit_bytes=mib * MIB)


def copy(source, target, sem):
    return pltpu.make_async_copy(source, target, sem)


def started(source, target, sem):
    moved = copy(source, target, sem)
    moved.start()
    return moved


def wait_all(ref, sem):
    copy(ref, ref, sem).wait()


def piece_of(ref, block, piece_rows, block_size):
    col_blocks = ref.shape[1] // block_size
    row = pl.multiple_of((block // col_blocks) * piece_rows, piece_rows)
    col = pl.multiple_of((block % col_blocks) * block_size, block_size)
    return ref.at[pl.ds(row, piece_rows), pl.ds(col, block_size)]


def rows_of(peer, piece_rows):
    return slice(peer * piece_rows, (peer + 1) * piece_rows)


def pack_kernel(
    places, order_ref, grad_ref, out_ref, here_ref, order_here, index_ref, sems, order_sem
):
    peers, slots, piece_rows, block_size = out_ref.shape
    table = started(order_ref, order_here, order_sem)
    col_blocks = grad_ref.shape[1] // block_size
    chunk_rows = grad_ref.shape[0] // sems.shape[0]
    loads = []
    for chunk in range(sems.shape[0]):
        rows = pl.ds(chunk * chunk_rows, chunk_rows)
        loads.append(started(grad_ref.at[rows], here_ref.at[rows], sems.at[chunk]))
    table.wait()
    for peer in range(peers):
        for slot in range(slots):
            index_ref[order_here[0, places[peer] * slots + slot]] = peer * slots + slot
    for chunk, load in enumerate(loads):
        load.wait()
        for row in range(chunk * chunk_rows, (chunk + 1) * chunk_rows, piece_rows):
            for column in range(col_blocks):
                at = index_ref[row // piece_rows * col_blocks + column]
                out_ref[at // slots, at % slots] = here_ref[
                    row : row + piece_rows, column * block_size : (column + 1) * block_size
                ]


def unpack_kernel(places, order_ref, moved_ref, out_ref, sem):
    peers, slots, piece_rows, block_size = moved_ref.shape
    for peer in range(peers):
        for slot in range(slots):
            block = order_ref[0, places[peer] * slots + slot]
            started(
                moved_ref.at[peer, slot], piece_of(out_ref, block, piece_rows, block_size), sem
            )
    wait_all(moved_ref, sem)


def sum_rows(x):
    return jnp.sum(x.reshape(-1, 8, x.shape[-1]), axis=0)


def mid_kernel(
    places, arrived_ref, second_ref, left_ref, right_ref, shampoo_ref, held_ref, sums_ref, low_ref, sem
):
    peers, slots, piece_rows, block_size = arrived_ref.shape
    half = block_size // 2
    half_peers = peers // 2
    kept = started(arrived_ref, held_ref, sem)
    adam_sq = jnp.zeros((8, block_size), F32)
    shampoo_sq = jnp.zeros((8, block_size), F32)
    for slot in range(slots):
        for peer in range(peers):
            rows = rows_of(places[peer], piece_rows)
            held = arrived_ref[peer, slot]
            low_ref[slot, rows, :] = held.astype(BF16)
            new_second = 0.99 * second_ref[slot, rows, :] + 0.01 * held * held
            adam = held / (jnp.sqrt(new_second) + 1e-08)
            adam_sq += sum_rows(adam * adam)
    for slot in range(slots):
        for part in range(2):
            rows = slice(part * half, (part + 1) * half)
            left_applied = jnp.dot(
                left_ref[slot, rows, :], low_ref[slot], preferred_element_type=F32
            ).astype(BF16)
            shampoo = jnp.dot(left_applied, right_ref[slot], preferred_element_type=F32)
            shampoo_ref[part * half_peers : (part + 1) * half_peers, slot] = shampoo.reshape(
                half_peers, piece_rows, block_size
            )
            shampoo_sq += sum_rows(shampoo * shampoo)
    ranks = sums_ref.shape[0]
    sums_ref[:, 0, :] = jnp.full((ranks, 128), jnp.sum(adam_sq), F32)
    sums_ref[:, 1, :] = jnp.full((ranks, 128), jnp.sum(shampoo_sq), F32)
    kept.wait()


def graft_of(sums_ref):
    root = jnp.sqrt(jnp.sum(sums_ref[...], axis=0))
    return root[0:1, 0:1] / (root[1:2, 0:1] + 1e-06)


def step_kernel(places, sums_ref, shampoo_ref, momentum_ref, step_ref, here_ref, sem):
    peers, slots, piece_rows, block_size = shampoo_ref.shape
    graft = graft_of(sums_ref)
    count = peers // (2 * CHUNKS)
    for peer in range(peers):
        rows = rows_of(places[peer], piece_rows)
        for slot in range(slots):
            scaled = graft * shampoo_ref[places[peer], slot]
            new_momentum = 0.9 * momentum_ref[slot, rows, :] + scaled
            here_ref[peer, slot] = -(0.9 * new_momentum + scaled)
        if peer % count == count - 1:
            part = pl.ds(peer - count + 1, count)
            started(here_ref.at[part], step_ref.at[part], sem)
    wait_all(here_ref, sem)


def rest_kernel(
    out_places, back_places, held_ref, second_ref, left_ref, right_ref, momentum_ref, step_ref,
    new_left_ref, new_right_ref, new_second_ref, new_momentum_ref,
    held_here, second_here, left_here, right_here, momentum_here, step_here, high_ref, low_ref,
    sems, store_sem,
):
    peers, slots, piece_rows, block_size = held_ref.shape
    loads = []
    for slot in range(slots):
        pairs = (
            (left_ref.at[slot], left_here.at[slot]),
            (right_ref.at[slot], right_here.at[slot]),
            (second_ref.at[slot], second_here.at[slot]),
            (momentum_ref.at[slot], momentum_here.at[slot]),
            (step_ref.at[:, slot], step_here.at[:, slot]),
            (held_ref.at[:, slot], held_here.at[:, slot]),
        )[::-1]
        loads.append([started(*pair, sems.at[slot, k]) for k, pair in enumerate(pairs)])
    scale = 0.1 / block_size
    half = block_size // 2
    for slot in range(slots):
        loads[slot][0].wait()
        for peer in range(peers):
            rows = rows_of(out_places[peer], piece_rows)
            held = held_here[peer, slot]
            high = held.astype(BF16)
            high_ref[slot, rows, :] = high
            low_ref[slot, rows, :] = (held - high.astype(F32)).astype(BF16)
        for k, (here, ref) in enumerate(
            ((left_here, new_left_ref), (right_here, new_right_ref))
        ):
            product = functools.partial(
                lax.dot_general,
                dimension_numbers=(((1 - k,), (1 - k,)), ((), ())),
                preferred_element_type=F32,
            )
            loads[slot][5 - k].wait()
            for part in range(2):
                cut = slice(part * half, (part + 1) * half)
                at = (slot, cut, slice(None)) if k == 0 else (slot, slice(None), cut)
                gram = (
                    product(high_ref[at], low_ref[slot])
                    + product(low_ref[at], high_ref[slot])
                    + product(high_ref[at], high_ref[slot])
                )
                here[slot, cut, :] = 0.9 * here[slot, cut, :] + scale * gram
            started(here.at[slot], ref.at[slot], store_sem)
        for load in loads[slot][1:4]:
            load.wait()
        for peer in range(peers):
            rows = rows_of(out_places[peer], piece_rows)
            held = held_here[peer, slot]
            second_here[slot, rows, :] = 0.99 * second_here[slot, rows, :] + 0.01 * held * held
            rows = rows_of(back_places[peer], piece_rows)
            momentum_here[slot, rows, :] = (
                0.9 * momentum_here[slot, rows, :] - step_here[peer, slot]
            ) * (1.0 / 1.9)
        started(second_here.at[slot], new_second_ref.at[slot], store_sem)
        started(momentum_here.at[slot], new_momentum_ref.at[slot], store_sem)
    for here in (left_here, right_here, second_here, momentum_here):
        wait_all(here, store_sem)


def body(grad, owner_order, left_stat, right_stat, left_root, right_root, momentum, second):
    slots, block_size = left_stat.shape[0], left_stat.shape[1]
    peers, ranks = lax.axis_size(TENSOR), lax.axis_size(DP + TENSOR)
    out_places, back_places = places_of(OUT_ORDER), places_of(BACK_ORDER)
    piece_rows = block_size // peers
    pair = (peers, slots, piece_rows, block_size)
    blocks = (slots, block_size, block_size)
    hbm = lambda shape: pltpu.HBM(shape, F32)
    vmem = lambda shape, dtype=F32: pltpu.VMEM(shape, dtype)
    exchange = functools.partial(lax.all_to_all, split_axis=0, concat_axis=0, tiled=True)
    order = in_hbm(owner_order)

    outgoing = pl.pallas_call(
        functools.partial(pack_kernel, out_places),
        out_shape=vmem(pair),
        in_specs=[ANY, ANY],
        out_specs=VMEM,
        scratch_shapes=[
            vmem(grad.shape), pltpu.SMEM(owner_order.shape, jnp.int32),
            pltpu.SMEM((peers * slots,), jnp.int32), DMA((2 * CHUNKS,)), DMA,
        ],
        compiler_params=params(8),
        name="pack",
    )(order, in_hbm(grad))
    arrived = exchange(outgoing, OUT_ORDER)

    shampoo, held, sums = pl.pallas_call(
        functools.partial(mid_kernel, out_places),
        out_shape=(vmem(pair), hbm(pair), jax.ShapeDtypeStruct((ranks, 2, 128), F32)),
        in_specs=[VMEM] * 4,
        out_specs=(VMEM, ANY, VMEM),
        scratch_shapes=[vmem(blocks, BF16), DMA],
        compiler_params=params(16),
        name="mid",
    )(in_vmem(arrived), in_vmem(second), in_vmem(left_root), in_vmem(right_root))
    sums = exchange(sums, DP + TENSOR)

    step = pl.pallas_call(
        functools.partial(step_kernel, back_places),
        out_shape=hbm(pair),
        in_specs=[VMEM] * 3,
        out_specs=ANY,
        scratch_shapes=[vmem(pair), DMA],
        compiler_params=params(8),
        name="step",
    )(sums, in_vmem(shampoo), in_vmem(momentum))
    returned = exchange(step, BACK_ORDER)

    new_left, new_right, new_second, new_momentum = pl.pallas_call(
        functools.partial(rest_kernel, out_places, back_places),
        out_shape=(hbm(blocks),) * 4,
        in_specs=[ANY] * 6,
        out_specs=(ANY,) * 4,
        scratch_shapes=[vmem(pair)] + [vmem(blocks)] * 4 + [vmem(pair)]
        + [vmem(blocks, BF16)] * 2 + [DMA((slots, 6)), DMA],
        compiler_params=params(24),
        cost_estimate=pl.CostEstimate(
            flops=slots * 12 * block_size**3, bytes_accessed=18 * MIB, transcendentals=0
        ),
        name="rest",
    )(
        in_hbm(held), in_hbm(second), in_hbm(left_stat), in_hbm(right_stat),
        in_hbm(momentum), in_hbm(step),
    )

    update = pl.pallas_call(
        functools.partial(unpack_kernel, back_places),
        out_shape=hbm(grad.shape),
        in_specs=[pl.BlockSpec(memory_space=pltpu.SMEM), VMEM],
        out_specs=ANY,
        scratch_shapes=[DMA],
        compiler_params=params(8),
        name="unpack",
    )(order, in_vmem(returned))
    return (new_left, new_right, new_momentum, new_second, update)


def solution(mesh):
    names, sizes = zip(*FINE)
    fine = jax.sharding.Mesh(mesh.devices.reshape(sizes), names)
    owned = P(DP + TENSOR, None, None)
    return jax.shard_map(
        body,
        mesh=fine,
        in_specs=(P(TENSOR, DP), P(DP, None)) + (owned,) * 6,
        out_specs=(owned,) * 4 + (P(TENSOR, DP),),
        check_vma=False,
    )
```

```python
import functools

import jax
import jax.numpy as jnp
import numpy as np
from jax import lax
from jax.experimental import pallas as pl
from jax.experimental.pallas import tpu as pltpu
from jax.sharding import PartitionSpec as P

ANY = pl.BlockSpec(memory_space=pl.ANY)
VMEM = pl.BlockSpec(memory_space=pltpu.VMEM)
DMA = pltpu.SemaphoreType.DMA
MIB = 1 << 20
F32 = jnp.float32
BF16 = jnp.bfloat16
CHUNKS = 4


FINE = (("z", 4), ("yh", 2), ("x", 4), ("yl", 2), ("core", 2))
DP, TENSOR = ("z", "yh"), ("x", "yl", "core")
OUT_ORDER, BACK_ORDER = TENSOR, TENSOR


def places_of(order):
    sizes = dict(FINE)
    places = []
    for at in np.ndindex(*(sizes[axis] for axis in order)):
        where = dict(zip(order, at))
        place = 0
        for axis in TENSOR:
            place = place * sizes[axis] + where[axis]
        places.append(place)
    return places


def in_vmem(x):
    return pltpu.with_memory_space_constraint(x, pltpu.VMEM)


def in_hbm(x):
    return pltpu.with_memory_space_constraint(x, pltpu.HBM)


def params(mib):
    return pltpu.CompilerParams(vmem_limit_bytes=mib * MIB)


def copy(source, target, sem):
    return pltpu.make_async_copy(source, target, sem)


def started(source, target, sem):
    moved = copy(source, target, sem)
    moved.start()
    return moved


def wait_all(ref, sem):
    copy(ref, ref, sem).wait()


def piece_of(ref, block, piece_rows, block_size):
    col_blocks = ref.shape[1] // block_size
    row = pl.multiple_of((block // col_blocks) * piece_rows, piece_rows)
    col = pl.multiple_of((block % col_blocks) * block_size, block_size)
    return ref.at[pl.ds(row, piece_rows), pl.ds(col, block_size)]


def rows_of(peer, piece_rows):
    return slice(peer * piece_rows, (peer + 1) * piece_rows)


def pack_kernel(
    places, order_ref, grad_ref, out_ref, here_ref, order_here, index_ref, sems, order_sem
):
    peers, slots, piece_rows, block_size = out_ref.shape
    table = started(order_ref, order_here, order_sem)
    col_blocks = grad_ref.shape[1] // block_size
    chunk_rows = grad_ref.shape[0] // sems.shape[0]
    loads = []
    for chunk in range(sems.shape[0]):
        rows = pl.ds(chunk * chunk_rows, chunk_rows)
        loads.append(started(grad_ref.at[rows], here_ref.at[rows], sems.at[chunk]))
    table.wait()
    for peer in range(peers):
        for slot in range(slots):
            index_ref[order_here[0, places[peer] * slots + slot]] = peer * slots + slot
    for chunk, load in enumerate(loads):
        load.wait()
        for row in range(chunk * chunk_rows, (chunk + 1) * chunk_rows, piece_rows):
            for column in range(col_blocks):
                at = index_ref[row // piece_rows * col_blocks + column]
                out_ref[at // slots, at % slots] = here_ref[
                    row : row + piece_rows, column * block_size : (column + 1) * block_size
                ]


def unpack_kernel(places, order_ref, moved_ref, out_ref, sem):
    peers, slots, piece_rows, block_size = moved_ref.shape
    for peer in range(peers):
        for slot in range(slots):
            block = order_ref[0, places[peer] * slots + slot]
            started(
                moved_ref.at[peer, slot], piece_of(out_ref, block, piece_rows, block_size), sem
            )
    wait_all(moved_ref, sem)


def sum_rows(x):
    return jnp.sum(x.reshape(-1, 8, x.shape[-1]), axis=0)


def mid_kernel(
    places, arrived_ref, second_ref, left_ref, right_ref, shampoo_ref, held_ref, sums_ref, low_ref, sem
):
    peers, slots, piece_rows, block_size = arrived_ref.shape
    half = block_size // 2
    half_peers = peers // 2
    kept = started(arrived_ref, held_ref, sem)
    row_order = sorted(range(peers), key=lambda peer: places[peer])

    adam_sq = jnp.zeros((8, block_size), F32)
    shampoo_sq = jnp.zeros((8, block_size), F32)
    for slot in range(slots):
        for peer in row_order:
            rows = rows_of(places[peer], piece_rows)
            held = arrived_ref[peer, slot]
            low_ref[slot, rows, :] = held.astype(BF16)
            new_second = 0.99 * second_ref[slot, rows, :] + 0.01 * held * held
            adam = held * pl.reciprocal(jnp.sqrt(new_second) + 1e-08)
            adam_sq += sum_rows(adam * adam)
        for part in range(2):
            rows = slice(part * half, (part + 1) * half)
            left_applied = jnp.dot(
                left_ref[slot, rows, :], low_ref[slot], preferred_element_type=F32
            ).astype(BF16)
            shampoo = jnp.dot(left_applied, right_ref[slot], preferred_element_type=F32)
            shampoo_ref[part * half_peers : (part + 1) * half_peers, slot] = shampoo.reshape(
                half_peers, piece_rows, block_size
            )
            shampoo_sq += sum_rows(shampoo * shampoo)
    first = lax.broadcasted_iota(jnp.int32, (2, 128), 0) == 0
    sums = jnp.where(first, jnp.sum(adam_sq), jnp.sum(shampoo_sq))
    sums_ref[...] = jnp.broadcast_to(sums[None], sums_ref.shape)
    kept.wait()


def graft_of(sums_ref):
    root = jnp.sqrt(jnp.sum(sums_ref[...], axis=0))
    return root[0:1, 0:1] / (root[1:2, 0:1] + 1e-06)


def step_kernel(places, sums_ref, shampoo_ref, momentum_ref, step_ref, here_ref, sem):
    peers, slots, piece_rows, block_size = shampoo_ref.shape
    graft = graft_of(sums_ref)
    count = peers // (2 * CHUNKS)
    for peer in range(peers):
        rows = rows_of(places[peer], piece_rows)
        for slot in range(slots):
            scaled = graft * shampoo_ref[places[peer], slot]
            new_momentum = 0.9 * momentum_ref[slot, rows, :] + scaled
            here_ref[peer, slot] = -(0.9 * new_momentum + scaled)
        if peer % count == count - 1:
            part = pl.ds(peer - count + 1, count)
            started(here_ref.at[part], step_ref.at[part], sem)
    wait_all(here_ref, sem)


def rest_kernel(
    out_places, back_places, held_ref, second_ref, left_ref, right_ref, momentum_ref, step_ref,
    new_left_ref, new_right_ref, new_second_ref, new_momentum_ref,
    held_here, second_here, left_here, right_here, momentum_here, step_here, high_ref, low_ref,
    sems, store_sem,
):
    peers, slots, piece_rows, block_size = held_ref.shape
    loads = []
    for slot in range(slots):
        pairs = (
            (left_ref.at[slot], left_here.at[slot]),
            (right_ref.at[slot], right_here.at[slot]),
            (second_ref.at[slot], second_here.at[slot]),
            (momentum_ref.at[slot], momentum_here.at[slot]),
            (step_ref.at[:, slot], step_here.at[:, slot]),
            (held_ref.at[:, slot], held_here.at[:, slot]),
        )[::-1]
        loads.append([started(*pair, sems.at[slot, k]) for k, pair in enumerate(pairs)])
    scale = 0.1 / block_size
    half = block_size // 2
    for slot in range(slots):
        loads[slot][0].wait()
        for peer in range(peers):
            rows = rows_of(out_places[peer], piece_rows)
            held = held_here[peer, slot]
            high = held.astype(BF16)
            high_ref[slot, rows, :] = high
            low_ref[slot, rows, :] = (held - high.astype(F32)).astype(BF16)
        for k, (here, ref) in enumerate(
            ((left_here, new_left_ref), (right_here, new_right_ref))
        ):
            product = functools.partial(
                lax.dot_general,
                dimension_numbers=(((1 - k,), (1 - k,)), ((), ())),
                preferred_element_type=F32,
            )
            loads[slot][5 - k].wait()
            for part in range(2):
                cut = slice(part * half, (part + 1) * half)
                at = (slot, cut, slice(None)) if k == 0 else (slot, slice(None), cut)
                gram = (
                    product(high_ref[at], low_ref[slot])
                    + product(low_ref[at], high_ref[slot])
                    + product(high_ref[at], high_ref[slot])
                )
                here[slot, cut, :] = 0.9 * here[slot, cut, :] + scale * gram
            started(here.at[slot], ref.at[slot], store_sem)
        for load in loads[slot][1:4]:
            load.wait()
        for peer in range(peers):
            rows = rows_of(out_places[peer], piece_rows)
            held = held_here[peer, slot]
            second_here[slot, rows, :] = 0.99 * second_here[slot, rows, :] + 0.01 * held * held
            rows = rows_of(back_places[peer], piece_rows)
            momentum_here[slot, rows, :] = (
                0.9 * momentum_here[slot, rows, :] - step_here[peer, slot]
            ) * (1.0 / 1.9)
        started(second_here.at[slot], new_second_ref.at[slot], store_sem)
        started(momentum_here.at[slot], new_momentum_ref.at[slot], store_sem)
    for here in (left_here, right_here, second_here, momentum_here):
        wait_all(here, store_sem)


def body(grad, owner_order, left_stat, right_stat, left_root, right_root, momentum, second):
    slots, block_size = left_stat.shape[0], left_stat.shape[1]
    peers, ranks = lax.axis_size(TENSOR), lax.axis_size(DP + TENSOR)
    out_places, back_places = places_of(OUT_ORDER), places_of(BACK_ORDER)
    piece_rows = block_size // peers
    pair = (peers, slots, piece_rows, block_size)
    blocks = (slots, block_size, block_size)
    hbm = lambda shape: pltpu.HBM(shape, F32)
    vmem = lambda shape, dtype=F32: pltpu.VMEM(shape, dtype)
    exchange = functools.partial(lax.all_to_all, split_axis=0, concat_axis=0, tiled=True)
    order = in_hbm(owner_order)

    outgoing = pl.pallas_call(
        functools.partial(pack_kernel, out_places),
        out_shape=vmem(pair),
        in_specs=[ANY, ANY],
        out_specs=VMEM,
        scratch_shapes=[
            vmem(grad.shape), pltpu.SMEM(owner_order.shape, jnp.int32),
            pltpu.SMEM((peers * slots,), jnp.int32), DMA((2 * CHUNKS,)), DMA,
        ],
        compiler_params=params(8),
        name="pack",
    )(order, in_hbm(grad))
    arrived = exchange(outgoing, OUT_ORDER)

    shampoo, held, sums = pl.pallas_call(
        functools.partial(mid_kernel, out_places),
        out_shape=(vmem(pair), hbm(pair), jax.ShapeDtypeStruct((ranks, 2, 128), F32)),
        in_specs=[VMEM] * 4,
        out_specs=(VMEM, ANY, VMEM),
        scratch_shapes=[vmem(blocks, BF16), DMA],
        compiler_params=params(16),
        name="mid",
    )(in_vmem(arrived), in_vmem(second), in_vmem(left_root), in_vmem(right_root))
    sums = exchange(sums, DP + TENSOR)

    step = pl.pallas_call(
        functools.partial(step_kernel, back_places),
        out_shape=hbm(pair),
        in_specs=[VMEM] * 3,
        out_specs=ANY,
        scratch_shapes=[vmem(pair), DMA],
        compiler_params=params(8),
        name="step",
    )(sums, in_vmem(shampoo), in_vmem(momentum))
    returned = exchange(step, BACK_ORDER)

    new_left, new_right, new_second, new_momentum = pl.pallas_call(
        functools.partial(rest_kernel, out_places, back_places),
        out_shape=(hbm(blocks),) * 4,
        in_specs=[ANY] * 6,
        out_specs=(ANY,) * 4,
        scratch_shapes=[vmem(pair)] + [vmem(blocks)] * 4 + [vmem(pair)]
        + [vmem(blocks, BF16)] * 2 + [DMA((slots, 6)), DMA],
        compiler_params=params(24),
        cost_estimate=pl.CostEstimate(
            flops=slots * 12 * block_size**3, bytes_accessed=18 * MIB, transcendentals=0
        ),
        name="rest",
    )(
        in_hbm(held), in_hbm(second), in_hbm(left_stat), in_hbm(right_stat),
        in_hbm(momentum), in_hbm(step),
    )

    update = pl.pallas_call(
        functools.partial(unpack_kernel, back_places),
        out_shape=hbm(grad.shape),
        in_specs=[pl.BlockSpec(memory_space=pltpu.SMEM), VMEM],
        out_specs=ANY,
        scratch_shapes=[DMA],
        compiler_params=params(8),
        name="unpack",
    )(order, in_vmem(returned))
    return (new_left, new_right, new_momentum, new_second, update)


def solution(mesh):
    names, sizes = zip(*FINE)
    fine = jax.sharding.Mesh(mesh.devices.reshape(sizes), names)
    owned = P(DP + TENSOR, None, None)
    return jax.shard_map(
        body,
        mesh=fine,
        in_specs=(P(TENSOR, DP), P(DP, None)) + (owned,) * 6,
        out_specs=(owned,) * 4 + (P(TENSOR, DP),),
        check_vma=False,
    )
```

```python
import functools

import jax
import jax.numpy as jnp
import numpy as np
from jax import lax
from jax.experimental import pallas as pl
from jax.experimental.pallas import tpu as pltpu
from jax.sharding import PartitionSpec as P

ANY = pl.BlockSpec(memory_space=pl.ANY)
VMEM = pl.BlockSpec(memory_space=pltpu.VMEM)
DMA = pltpu.SemaphoreType.DMA
MIB = 1 << 20
F32 = jnp.float32
BF16 = jnp.bfloat16
CHUNKS = 4


FINE = (("z", 4), ("yh", 2), ("x", 4), ("yl", 2), ("core", 2))
DP, TENSOR = ("z", "yh"), ("x", "yl", "core")
OUT_ORDER, BACK_ORDER = TENSOR, TENSOR


def places_of(order):
    sizes = dict(FINE)
    places = []
    for at in np.ndindex(*(sizes[axis] for axis in order)):
        where = dict(zip(order, at))
        place = 0
        for axis in TENSOR:
            place = place * sizes[axis] + where[axis]
        places.append(place)
    return places


def in_vmem(x):
    return pltpu.with_memory_space_constraint(x, pltpu.VMEM)


def in_hbm(x):
    return pltpu.with_memory_space_constraint(x, pltpu.HBM)


def params(mib):
    return pltpu.CompilerParams(vmem_limit_bytes=mib * MIB)


def copy(source, target, sem):
    return pltpu.make_async_copy(source, target, sem)


def started(source, target, sem):
    moved = copy(source, target, sem)
    moved.start()
    return moved


def wait_all(ref, sem):
    copy(ref, ref, sem).wait()


def piece_of(ref, block, piece_rows, block_size):
    col_blocks = ref.shape[1] // block_size
    row = pl.multiple_of((block // col_blocks) * piece_rows, piece_rows)
    col = pl.multiple_of((block % col_blocks) * block_size, block_size)
    return ref.at[pl.ds(row, piece_rows), pl.ds(col, block_size)]


def rows_of(peer, piece_rows):
    return slice(peer * piece_rows, (peer + 1) * piece_rows)


def pack_kernel(
    places, order_ref, grad_ref, out_ref, here_ref, order_here, index_ref, sems, order_sem
):
    peers, slots, piece_rows, block_size = out_ref.shape
    table = started(order_ref, order_here, order_sem)
    col_blocks = grad_ref.shape[1] // block_size
    chunk_rows = grad_ref.shape[0] // sems.shape[0]
    loads = []
    for chunk in range(sems.shape[0]):
        rows = pl.ds(chunk * chunk_rows, chunk_rows)
        loads.append(started(grad_ref.at[rows], here_ref.at[rows], sems.at[chunk]))
    table.wait()
    for peer in range(peers):
        for slot in range(slots):
            index_ref[order_here[0, places[peer] * slots + slot]] = peer * slots + slot
    for chunk, load in enumerate(loads):
        load.wait()
        for row in range(chunk * chunk_rows, (chunk + 1) * chunk_rows, piece_rows):
            for column in range(col_blocks):
                at = index_ref[row // piece_rows * col_blocks + column]
                out_ref[at // slots, at % slots] = here_ref[
                    row : row + piece_rows, column * block_size : (column + 1) * block_size
                ]


def unpack_kernel(places, order_ref, moved_ref, out_ref, sem):
    peers, slots, piece_rows, block_size = moved_ref.shape
    for peer in range(peers):
        for slot in range(slots):
            block = order_ref[0, places[peer] * slots + slot]
            started(
                moved_ref.at[peer, slot], piece_of(out_ref, block, piece_rows, block_size), sem
            )
    wait_all(moved_ref, sem)


def sum_rows(x):
    return jnp.sum(x.reshape(-1, 8, x.shape[-1]), axis=0)


def mid_kernel(
    places, arrived_ref, second_ref, left_ref, right_ref, shampoo_ref, held_ref, sums_ref,
    low_ref, applied_ref, sem,
):
    peers, slots, piece_rows, block_size = arrived_ref.shape
    half = block_size // 2
    half_peers = peers // 2
    kept = started(arrived_ref, held_ref, sem)
    row_order = sorted(range(peers), key=lambda peer: places[peer])

    adam_sq = jnp.zeros((8, block_size), F32)
    shampoo_sq = jnp.zeros((8, block_size), F32)
    for slot in range(slots):
        for peer in row_order:
            rows = rows_of(places[peer], piece_rows)
            held = arrived_ref[peer, slot]
            low_ref[slot, rows, :] = held.astype(BF16)
            new_second = 0.99 * second_ref[slot, rows, :] + 0.01 * held * held
            adam = held * pl.reciprocal(jnp.sqrt(new_second) + 1e-08)
            adam_sq += sum_rows(adam * adam)
    for slot in range(slots):
        for part in range(2):
            rows = slice(part * half, (part + 1) * half)
            applied_ref[slot, rows, :] = jnp.dot(
                left_ref[slot, rows, :], low_ref[slot], preferred_element_type=F32
            ).astype(BF16)
    for slot in range(slots):
        for part in range(2):
            rows = slice(part * half, (part + 1) * half)
            shampoo = jnp.dot(
                applied_ref[slot, rows, :], right_ref[slot], preferred_element_type=F32
            )
            shampoo_ref[part * half_peers : (part + 1) * half_peers, slot] = shampoo.reshape(
                half_peers, piece_rows, block_size
            )
            shampoo_sq += sum_rows(shampoo * shampoo)
    first = lax.broadcasted_iota(jnp.int32, (2, 128), 0) == 0
    sums = jnp.where(first, jnp.sum(adam_sq), jnp.sum(shampoo_sq))
    sums_ref[...] = jnp.broadcast_to(sums[None], sums_ref.shape)
    kept.wait()


def graft_of(sums_ref):
    root = jnp.sqrt(jnp.sum(sums_ref[...], axis=0))
    return root[0:1, 0:1] / (root[1:2, 0:1] + 1e-06)


def step_kernel(places, sums_ref, shampoo_ref, momentum_ref, step_ref, here_ref, sem):
    peers, slots, piece_rows, block_size = shampoo_ref.shape
    graft = graft_of(sums_ref)
    count = peers // (2 * CHUNKS)
    for peer in range(peers):
        rows = rows_of(places[peer], piece_rows)
        for slot in range(slots):
            scaled = graft * shampoo_ref[places[peer], slot]
            new_momentum = 0.9 * momentum_ref[slot, rows, :] + scaled
            here_ref[peer, slot] = -(0.9 * new_momentum + scaled)
        if peer % count == count - 1:
            part = pl.ds(peer - count + 1, count)
            started(here_ref.at[part], step_ref.at[part], sem)
    wait_all(here_ref, sem)


def rest_kernel(
    out_places, back_places, held_ref, second_ref, left_ref, right_ref, momentum_ref, step_ref,
    new_left_ref, new_right_ref, new_second_ref, new_momentum_ref,
    held_here, second_here, left_here, right_here, momentum_here, step_here, high_ref, low_ref,
    sems, store_sem,
):
    peers, slots, piece_rows, block_size = held_ref.shape

    def load(slot):
        pairs = (
            (left_ref.at[slot], left_here.at[slot]),
            (right_ref.at[slot], right_here.at[slot]),
            (second_ref.at[slot], second_here.at[slot]),
            (momentum_ref.at[slot], momentum_here.at[slot]),
            (step_ref.at[:, slot], step_here.at[:, slot]),
            (held_ref.at[:, slot], held_here.at[:, slot]),
        )[::-1]
        return [started(*pair, sems.at[slot, k]) for k, pair in enumerate(pairs)]

    scale = 0.1 / block_size
    half = block_size // 2
    loads = [load(0)]
    for slot in range(slots):
        loads[slot][0].wait()
        for peer in range(peers):
            rows = rows_of(out_places[peer], piece_rows)
            held = held_here[peer, slot]
            high = held.astype(BF16)
            high_ref[slot, rows, :] = high
            low_ref[slot, rows, :] = (held - high.astype(F32)).astype(BF16)
        for k, (here, ref) in enumerate(
            ((left_here, new_left_ref), (right_here, new_right_ref))
        ):
            product = functools.partial(
                lax.dot_general,
                dimension_numbers=(((1 - k,), (1 - k,)), ((), ())),
                preferred_element_type=F32,
            )
            loads[slot][5 - k].wait()
            for part in range(2):
                cut = slice(part * half, (part + 1) * half)
                at = (slot, cut, slice(None)) if k == 0 else (slot, slice(None), cut)
                gram = (
                    product(high_ref[at], low_ref[slot])
                    + product(low_ref[at], high_ref[slot])
                    + product(high_ref[at], high_ref[slot])
                )
                here[slot, cut, :] = 0.9 * here[slot, cut, :] + scale * gram
            started(here.at[slot], ref.at[slot], store_sem)
        if slot + 1 < slots:
            loads.append(load(slot + 1))
        for pending in loads[slot][1:4]:
            pending.wait()
        for peer in range(peers):
            rows = rows_of(out_places[peer], piece_rows)
            held = held_here[peer, slot]
            second_here[slot, rows, :] = 0.99 * second_here[slot, rows, :] + 0.01 * held * held
            rows = rows_of(back_places[peer], piece_rows)
            momentum_here[slot, rows, :] = (
                0.9 * momentum_here[slot, rows, :] - step_here[peer, slot]
            ) * (1.0 / 1.9)
        started(second_here.at[slot], new_second_ref.at[slot], store_sem)
        started(momentum_here.at[slot], new_momentum_ref.at[slot], store_sem)
    for here in (left_here, right_here, second_here, momentum_here):
        wait_all(here, store_sem)


def body(grad, owner_order, left_stat, right_stat, left_root, right_root, momentum, second):
    slots, block_size = left_stat.shape[0], left_stat.shape[1]
    peers, ranks = lax.axis_size(TENSOR), lax.axis_size(DP + TENSOR)
    out_places, back_places = places_of(OUT_ORDER), places_of(BACK_ORDER)
    piece_rows = block_size // peers
    pair = (peers, slots, piece_rows, block_size)
    blocks = (slots, block_size, block_size)
    hbm = lambda shape: pltpu.HBM(shape, F32)
    vmem = lambda shape, dtype=F32: pltpu.VMEM(shape, dtype)
    exchange = functools.partial(lax.all_to_all, split_axis=0, concat_axis=0, tiled=True)
    order = in_hbm(owner_order)

    outgoing = pl.pallas_call(
        functools.partial(pack_kernel, out_places),
        out_shape=vmem(pair),
        in_specs=[ANY, ANY],
        out_specs=VMEM,
        scratch_shapes=[
            vmem(grad.shape), pltpu.SMEM(owner_order.shape, jnp.int32),
            pltpu.SMEM((peers * slots,), jnp.int32), DMA((2 * CHUNKS,)), DMA,
        ],
        compiler_params=params(8),
        name="pack",
    )(order, in_hbm(grad))
    arrived = exchange(outgoing, OUT_ORDER)

    shampoo, held, sums = pl.pallas_call(
        functools.partial(mid_kernel, out_places),
        out_shape=(vmem(pair), hbm(pair), jax.ShapeDtypeStruct((ranks, 2, 128), F32)),
        in_specs=[VMEM] * 4,
        out_specs=(VMEM, ANY, VMEM),
        scratch_shapes=[vmem(blocks, BF16), vmem(blocks, BF16), DMA],
        compiler_params=params(16),
        name="mid",
    )(in_vmem(arrived), in_vmem(second), in_vmem(left_root), in_vmem(right_root))
    sums = exchange(sums, DP + TENSOR)

    step = pl.pallas_call(
        functools.partial(step_kernel, back_places),
        out_shape=hbm(pair),
        in_specs=[VMEM] * 3,
        out_specs=ANY,
        scratch_shapes=[vmem(pair), DMA],
        compiler_params=params(8),
        name="step",
    )(sums, in_vmem(shampoo), in_vmem(momentum))
    returned = exchange(step, BACK_ORDER)

    new_left, new_right, new_second, new_momentum = pl.pallas_call(
        functools.partial(rest_kernel, out_places, back_places),
        out_shape=(hbm(blocks),) * 4,
        in_specs=[ANY] * 6,
        out_specs=(ANY,) * 4,
        scratch_shapes=[vmem(pair)] + [vmem(blocks)] * 4 + [vmem(pair)]
        + [vmem(blocks, BF16)] * 2 + [DMA((slots, 6)), DMA],
        compiler_params=params(24),
        cost_estimate=pl.CostEstimate(
            flops=slots * 12 * block_size**3, bytes_accessed=18 * MIB, transcendentals=0
        ),
        name="rest",
    )(
        in_hbm(held), in_hbm(second), in_hbm(left_stat), in_hbm(right_stat),
        in_hbm(momentum), in_hbm(step),
    )

    update = pl.pallas_call(
        functools.partial(unpack_kernel, back_places),
        out_shape=hbm(grad.shape),
        in_specs=[pl.BlockSpec(memory_space=pltpu.SMEM), VMEM],
        out_specs=ANY,
        scratch_shapes=[DMA],
        compiler_params=params(8),
        name="unpack",
    )(order, in_vmem(returned))
    return (new_left, new_right, new_momentum, new_second, update)


def solution(mesh):
    names, sizes = zip(*FINE)
    fine = jax.sharding.Mesh(mesh.devices.reshape(sizes), names)
    owned = P(DP + TENSOR, None, None)
    return jax.shard_map(
        body,
        mesh=fine,
        in_specs=(P(TENSOR, DP), P(DP, None)) + (owned,) * 6,
        out_specs=(owned,) * 4 + (P(TENSOR, DP),),
        check_vma=False,
    )
```

```python
import functools

import jax
import jax.numpy as jnp
import numpy as np
from jax import lax
from jax.experimental import pallas as pl
from jax.experimental.pallas import tpu as pltpu
from jax.sharding import PartitionSpec as P

ANY = pl.BlockSpec(memory_space=pl.ANY)
VMEM = pl.BlockSpec(memory_space=pltpu.VMEM)
DMA = pltpu.SemaphoreType.DMA
MIB = 1 << 20
F32 = jnp.float32
BF16 = jnp.bfloat16
CHUNKS = 4


FINE = (("z", 4), ("yh", 2), ("x", 4), ("yl", 2), ("core", 2))
DP, TENSOR = ("z", "yh"), ("x", "yl", "core")
OUT_ORDER, BACK_ORDER = TENSOR, TENSOR


def places_of(order):
    sizes = dict(FINE)
    places = []
    for at in np.ndindex(*(sizes[axis] for axis in order)):
        where = dict(zip(order, at))
        place = 0
        for axis in TENSOR:
            place = place * sizes[axis] + where[axis]
        places.append(place)
    return places


def in_vmem(x):
    return pltpu.with_memory_space_constraint(x, pltpu.VMEM)


def in_hbm(x):
    return pltpu.with_memory_space_constraint(x, pltpu.HBM)


def params(mib):
    return pltpu.CompilerParams(vmem_limit_bytes=mib * MIB)


def copy(source, target, sem):
    return pltpu.make_async_copy(source, target, sem)


def started(source, target, sem):
    moved = copy(source, target, sem)
    moved.start()
    return moved


def wait_all(ref, sem):
    copy(ref, ref, sem).wait()


def rows_of(peer, piece_rows):
    return slice(peer * piece_rows, (peer + 1) * piece_rows)


def put_index(places, slots, order_ref, index_ref):
    for peer, place in enumerate(places):
        for slot in range(slots):
            index_ref[order_ref[0, place * slots + slot]] = peer * slots + slot


def pack_kernel(
    places, order_ref, grad_ref, out_ref, here_ref, order_here, index_ref, sems, order_sem
):
    peers, slots, piece_rows, block_size = out_ref.shape
    table = started(order_ref, order_here, order_sem)
    col_blocks = grad_ref.shape[1] // block_size
    chunk_rows = grad_ref.shape[0] // sems.shape[0]
    loads = []
    for chunk in range(sems.shape[0]):
        rows = pl.ds(chunk * chunk_rows, chunk_rows)
        loads.append(started(grad_ref.at[rows], here_ref.at[rows], sems.at[chunk]))
    table.wait()
    put_index(places, slots, order_here, index_ref)
    for chunk, load in enumerate(loads):
        load.wait()
        for row in range(chunk * chunk_rows, (chunk + 1) * chunk_rows, piece_rows):
            for column in range(col_blocks):
                at = index_ref[row // piece_rows * col_blocks + column]
                out_ref[at // slots, at % slots] = here_ref[
                    row : row + piece_rows, column * block_size : (column + 1) * block_size
                ]


def unpack_kernel(places, order_ref, moved_ref, out_ref, here_ref, index_ref, sem):
    peers, slots, piece_rows, block_size = moved_ref.shape
    put_index(places, slots, order_ref, index_ref)
    col_blocks = out_ref.shape[1] // block_size
    chunk_rows = out_ref.shape[0] // (2 * CHUNKS)
    for start in range(0, out_ref.shape[0], chunk_rows):
        for row in range(start, start + chunk_rows, piece_rows):
            for column in range(col_blocks):
                at = index_ref[row // piece_rows * col_blocks + column]
                here_ref[
                    row : row + piece_rows, column * block_size : (column + 1) * block_size
                ] = moved_ref[at // slots, at % slots]
        rows = pl.ds(start, chunk_rows)
        started(here_ref.at[rows], out_ref.at[rows], sem)
    wait_all(here_ref, sem)


def sum_rows(x):
    return jnp.sum(x.reshape(-1, 8, x.shape[-1]), axis=0)


def mid_kernel(
    places, arrived_ref, second_ref, left_ref, right_ref, shampoo_ref, held_ref, sums_ref,
    low_ref, applied_ref, sem,
):
    peers, slots, piece_rows, block_size = arrived_ref.shape
    half = block_size // 2
    half_peers = peers // 2
    kept = started(arrived_ref, held_ref, sem)
    row_order = sorted(range(peers), key=lambda peer: places[peer])

    adam_sq = jnp.zeros((8, block_size), F32)
    shampoo_sq = jnp.zeros((8, block_size), F32)
    for slot in range(slots):
        for peer in row_order:
            rows = rows_of(places[peer], piece_rows)
            low_ref[slot, rows, :] = arrived_ref[peer, slot].astype(BF16)
    for slot in range(slots):
        for part in range(2):
            rows = slice(part * half, (part + 1) * half)
            applied_ref[slot, rows, :] = jnp.dot(
                left_ref[slot, rows, :], low_ref[slot], preferred_element_type=F32
            ).astype(BF16)
            for peer in row_order[part * half_peers : (part + 1) * half_peers]:
                rows = rows_of(places[peer], piece_rows)
                held = arrived_ref[peer, slot]
                new_second = 0.99 * second_ref[slot, rows, :] + 0.01 * held * held
                adam = held * pl.reciprocal(jnp.sqrt(new_second) + 1e-08)
                adam_sq += sum_rows(adam * adam)
    for slot in range(slots):
        for part in range(2):
            rows = slice(part * half, (part + 1) * half)
            shampoo = jnp.dot(
                applied_ref[slot, rows, :], right_ref[slot], preferred_element_type=F32
            )
            shampoo_ref[part * half_peers : (part + 1) * half_peers, slot] = shampoo.reshape(
                half_peers, piece_rows, block_size
            )
            shampoo_sq += sum_rows(shampoo * shampoo)
    first = lax.broadcasted_iota(jnp.int32, (2, 128), 0) == 0
    sums = jnp.where(first, jnp.sum(adam_sq), jnp.sum(shampoo_sq))
    sums_ref[...] = jnp.broadcast_to(sums[None], sums_ref.shape)
    kept.wait()


def graft_of(sums_ref):
    root = jnp.sqrt(jnp.sum(sums_ref[...], axis=0))
    return root[0:1, 0:1] / (root[1:2, 0:1] + 1e-06)


def step_kernel(places, sums_ref, shampoo_ref, momentum_ref, step_ref, here_ref, sem):
    peers, slots, piece_rows, block_size = shampoo_ref.shape
    graft = graft_of(sums_ref)
    count = peers // (2 * CHUNKS)
    for peer in range(peers):
        rows = rows_of(places[peer], piece_rows)
        for slot in range(slots):
            scaled = graft * shampoo_ref[places[peer], slot]
            new_momentum = 0.9 * momentum_ref[slot, rows, :] + scaled
            here_ref[peer, slot] = -(0.9 * new_momentum + scaled)
        if peer % count == count - 1:
            part = pl.ds(peer - count + 1, count)
            started(here_ref.at[part], step_ref.at[part], sem)
    wait_all(here_ref, sem)


def rest_kernel(
    out_places, back_places, held_ref, second_ref, left_ref, right_ref, momentum_ref, step_ref,
    new_left_ref, new_right_ref, new_second_ref, new_momentum_ref,
    held_here, second_here, left_here, right_here, momentum_here, step_here, high_ref, low_ref,
    sems, store_sem,
):
    peers, slots, piece_rows, block_size = held_ref.shape

    def load(slot):
        pairs = (
            (left_ref.at[slot], left_here.at[slot]),
            (right_ref.at[slot], right_here.at[slot]),
            (second_ref.at[slot], second_here.at[slot]),
            (momentum_ref.at[slot], momentum_here.at[slot]),
            (step_ref.at[:, slot], step_here.at[:, slot]),
            (held_ref.at[:, slot], held_here.at[:, slot]),
        )[::-1]
        return [started(*pair, sems.at[slot, k]) for k, pair in enumerate(pairs)]

    scale = 0.1 / block_size
    half = block_size // 2
    loads = [load(0)]
    for slot in range(slots):
        loads[slot][0].wait()
        for peer in range(peers):
            rows = rows_of(out_places[peer], piece_rows)
            held = held_here[peer, slot]
            high = held.astype(BF16)
            high_ref[slot, rows, :] = high
            low_ref[slot, rows, :] = (held - high.astype(F32)).astype(BF16)
        for k, (here, ref) in enumerate(
            ((left_here, new_left_ref), (right_here, new_right_ref))
        ):
            product = functools.partial(
                lax.dot_general,
                dimension_numbers=(((1 - k,), (1 - k,)), ((), ())),
                preferred_element_type=F32,
            )
            loads[slot][5 - k].wait()
            for part in range(2):
                cut = slice(part * half, (part + 1) * half)
                at = (slot, cut, slice(None)) if k == 0 else (slot, slice(None), cut)
                gram = (
                    product(high_ref[at], low_ref[slot])
                    + product(low_ref[at], high_ref[slot])
                    + product(high_ref[at], high_ref[slot])
                )
                here[slot, cut, :] = 0.9 * here[slot, cut, :] + scale * gram
            started(here.at[slot], ref.at[slot], store_sem)
        if slot + 1 < slots:
            loads.append(load(slot + 1))
        for pending in loads[slot][1:4]:
            pending.wait()
        for peer in range(peers):
            rows = rows_of(out_places[peer], piece_rows)
            held = held_here[peer, slot]
            second_here[slot, rows, :] = 0.99 * second_here[slot, rows, :] + 0.01 * held * held
            rows = rows_of(back_places[peer], piece_rows)
            momentum_here[slot, rows, :] = (
                0.9 * momentum_here[slot, rows, :] - step_here[peer, slot]
            ) * (1.0 / 1.9)
        started(second_here.at[slot], new_second_ref.at[slot], store_sem)
        started(momentum_here.at[slot], new_momentum_ref.at[slot], store_sem)
    for here in (left_here, right_here, second_here, momentum_here):
        wait_all(here, store_sem)


def body(grad, owner_order, left_stat, right_stat, left_root, right_root, momentum, second):
    slots, block_size = left_stat.shape[0], left_stat.shape[1]
    peers, ranks = lax.axis_size(TENSOR), lax.axis_size(DP + TENSOR)
    out_places, back_places = places_of(OUT_ORDER), places_of(BACK_ORDER)
    piece_rows = block_size // peers
    pair = (peers, slots, piece_rows, block_size)
    blocks = (slots, block_size, block_size)
    hbm = lambda shape: pltpu.HBM(shape, F32)
    vmem = lambda shape, dtype=F32: pltpu.VMEM(shape, dtype)
    exchange = functools.partial(lax.all_to_all, split_axis=0, concat_axis=0, tiled=True)
    order = in_hbm(owner_order)

    outgoing = pl.pallas_call(
        functools.partial(pack_kernel, out_places),
        out_shape=vmem(pair),
        in_specs=[ANY, ANY],
        out_specs=VMEM,
        scratch_shapes=[
            vmem(grad.shape), pltpu.SMEM(owner_order.shape, jnp.int32),
            pltpu.SMEM((peers * slots,), jnp.int32), DMA((2 * CHUNKS,)), DMA,
        ],
        compiler_params=params(8),
        name="pack",
    )(order, in_hbm(grad))
    arrived = exchange(outgoing, OUT_ORDER)

    shampoo, held, sums = pl.pallas_call(
        functools.partial(mid_kernel, out_places),
        out_shape=(vmem(pair), hbm(pair), jax.ShapeDtypeStruct((ranks, 2, 128), F32)),
        in_specs=[VMEM] * 4,
        out_specs=(VMEM, ANY, VMEM),
        scratch_shapes=[vmem(blocks, BF16), vmem(blocks, BF16), DMA],
        compiler_params=params(16),
        name="mid",
    )(in_vmem(arrived), in_vmem(second), in_vmem(left_root), in_vmem(right_root))
    sums = exchange(sums, DP + TENSOR)

    step = pl.pallas_call(
        functools.partial(step_kernel, back_places),
        out_shape=hbm(pair),
        in_specs=[VMEM] * 3,
        out_specs=ANY,
        scratch_shapes=[vmem(pair), DMA],
        compiler_params=params(8),
        name="step",
    )(sums, in_vmem(shampoo), in_vmem(momentum))
    returned = exchange(step, BACK_ORDER)

    new_left, new_right, new_second, new_momentum = pl.pallas_call(
        functools.partial(rest_kernel, out_places, back_places),
        out_shape=(hbm(blocks),) * 4,
        in_specs=[ANY] * 6,
        out_specs=(ANY,) * 4,
        scratch_shapes=[vmem(pair)] + [vmem(blocks)] * 4 + [vmem(pair)]
        + [vmem(blocks, BF16)] * 2 + [DMA((slots, 6)), DMA],
        compiler_params=params(24),
        cost_estimate=pl.CostEstimate(
            flops=slots * 12 * block_size**3, bytes_accessed=18 * MIB, transcendentals=0
        ),
        name="rest",
    )(
        in_hbm(held), in_hbm(second), in_hbm(left_stat), in_hbm(right_stat),
        in_hbm(momentum), in_hbm(step),
    )

    update = pl.pallas_call(
        functools.partial(unpack_kernel, back_places),
        out_shape=hbm(grad.shape),
        in_specs=[pl.BlockSpec(memory_space=pltpu.SMEM), VMEM],
        out_specs=ANY,
        scratch_shapes=[vmem(grad.shape), pltpu.SMEM((peers * slots,), jnp.int32), DMA],
        compiler_params=params(8),
        name="unpack",
    )(order, in_vmem(returned))
    return (new_left, new_right, new_momentum, new_second, update)


def solution(mesh):
    names, sizes = zip(*FINE)
    fine = jax.sharding.Mesh(mesh.devices.reshape(sizes), names)
    owned = P(DP + TENSOR, None, None)
    return jax.shard_map(
        body,
        mesh=fine,
        in_specs=(P(TENSOR, DP), P(DP, None)) + (owned,) * 6,
        out_specs=(owned,) * 4 + (P(TENSOR, DP),),
        check_vma=False,
    )
```

```python
import functools

import jax
import jax.numpy as jnp
import numpy as np
from jax import lax
from jax.experimental import pallas as pl
from jax.experimental.pallas import tpu as pltpu
from jax.sharding import PartitionSpec as P

ANY = pl.BlockSpec(memory_space=pl.ANY)
VMEM = pl.BlockSpec(memory_space=pltpu.VMEM)
DMA = pltpu.SemaphoreType.DMA
MIB = 1 << 20
F32 = jnp.float32
BF16 = jnp.bfloat16
CHUNKS = 4


FINE = (("z", 4), ("yh", 2), ("x", 4), ("yl", 2), ("core", 2))
DP, TENSOR = ("z", "yh"), ("x", "yl", "core")
OUT_ORDER, BACK_ORDER = TENSOR, TENSOR


def places_of(order):
    sizes = dict(FINE)
    places = []
    for at in np.ndindex(*(sizes[axis] for axis in order)):
        where = dict(zip(order, at))
        place = 0
        for axis in TENSOR:
            place = place * sizes[axis] + where[axis]
        places.append(place)
    return places


def in_vmem(x):
    return pltpu.with_memory_space_constraint(x, pltpu.VMEM)


def in_hbm(x):
    return pltpu.with_memory_space_constraint(x, pltpu.HBM)


def params(mib):
    return pltpu.CompilerParams(vmem_limit_bytes=mib * MIB)


def copy(source, target, sem):
    return pltpu.make_async_copy(source, target, sem)


def started(source, target, sem):
    moved = copy(source, target, sem)
    moved.start()
    return moved


def wait_all(ref, sem):
    copy(ref, ref, sem).wait()


def piece_of(ref, block, piece_rows, block_size):
    col_blocks = ref.shape[1] // block_size
    row = pl.multiple_of((block // col_blocks) * piece_rows, piece_rows)
    col = pl.multiple_of((block % col_blocks) * block_size, block_size)
    return ref.at[pl.ds(row, piece_rows), pl.ds(col, block_size)]


def rows_of(peer, piece_rows):
    return slice(peer * piece_rows, (peer + 1) * piece_rows)


def pack_kernel(
    places, order_ref, grad_ref, out_ref, here_ref, order_here, index_ref, sems, order_sem
):
    peers, slots, piece_rows, block_size = out_ref.shape
    table = started(order_ref, order_here, order_sem)
    col_blocks = grad_ref.shape[1] // block_size
    chunk_rows = grad_ref.shape[0] // sems.shape[0]
    loads = []
    for chunk in range(sems.shape[0]):
        rows = pl.ds(chunk * chunk_rows, chunk_rows)
        loads.append(started(grad_ref.at[rows], here_ref.at[rows], sems.at[chunk]))
    table.wait()
    for peer in range(peers):
        for slot in range(slots):
            index_ref[order_here[0, places[peer] * slots + slot]] = peer * slots + slot
    for chunk, load in enumerate(loads):
        load.wait()
        for row in range(chunk * chunk_rows, (chunk + 1) * chunk_rows, piece_rows):
            for column in range(col_blocks):
                at = index_ref[row // piece_rows * col_blocks + column]
                out_ref[at // slots, at % slots] = here_ref[
                    row : row + piece_rows, column * block_size : (column + 1) * block_size
                ]


def unpack_kernel(places, order_ref, moved_ref, out_ref, sem):
    peers, slots, piece_rows, block_size = moved_ref.shape
    for peer in range(peers):
        for slot in range(slots):
            block = order_ref[0, places[peer] * slots + slot]
            started(
                moved_ref.at[peer, slot], piece_of(out_ref, block, piece_rows, block_size), sem
            )
    wait_all(moved_ref, sem)


def sum_rows(x):
    return jnp.sum(x.reshape(-1, 8, x.shape[-1]), axis=0)


def mid_kernel(
    places, arrived_ref, second_ref, left_ref, right_ref, shampoo_ref, held_ref, sums_ref,
    low_ref, applied_ref, sem,
):
    peers, slots, piece_rows, block_size = arrived_ref.shape
    kept = started(arrived_ref, held_ref, sem)
    row_order = sorted(range(peers), key=lambda peer: places[peer])

    adam_sq = jnp.zeros((8, block_size), F32)
    shampoo_sq = jnp.zeros((8, block_size), F32)
    for slot in range(slots):
        for peer in row_order:
            rows = rows_of(places[peer], piece_rows)
            held = arrived_ref[peer, slot]
            low_ref[slot, rows, :] = held.astype(BF16)
            new_second = 0.99 * second_ref[slot, rows, :] + 0.01 * held * held
            adam = held * pl.reciprocal(jnp.sqrt(new_second) + 1e-08)
            adam_sq += sum_rows(adam * adam)
    for slot in range(slots):
        applied_ref[slot] = jnp.dot(
            left_ref[slot], low_ref[slot], preferred_element_type=F32
        ).astype(BF16)
    for slot in range(slots):
        shampoo = jnp.dot(applied_ref[slot], right_ref[slot], preferred_element_type=F32)
        shampoo_ref[:, slot] = shampoo.reshape(peers, piece_rows, block_size)
        shampoo_sq += sum_rows(shampoo * shampoo)
    first = lax.broadcasted_iota(jnp.int32, (2, 128), 0) == 0
    sums = jnp.where(first, jnp.sum(adam_sq), jnp.sum(shampoo_sq))
    sums_ref[...] = jnp.broadcast_to(sums[None], sums_ref.shape)
    kept.wait()


def graft_of(sums_ref):
    root = jnp.sqrt(jnp.sum(sums_ref[...], axis=0))
    return root[0:1, 0:1] / (root[1:2, 0:1] + 1e-06)


def step_kernel(places, sums_ref, shampoo_ref, momentum_ref, step_ref, here_ref, sem):
    peers, slots, piece_rows, block_size = shampoo_ref.shape
    graft = graft_of(sums_ref)
    count = peers // (2 * CHUNKS)
    for peer in range(peers):
        rows = rows_of(places[peer], piece_rows)
        for slot in range(slots):
            scaled = graft * shampoo_ref[places[peer], slot]
            new_momentum = 0.9 * momentum_ref[slot, rows, :] + scaled
            here_ref[peer, slot] = -(0.9 * new_momentum + scaled)
        if peer % count == count - 1:
            part = pl.ds(peer - count + 1, count)
            started(here_ref.at[part], step_ref.at[part], sem)
    wait_all(here_ref, sem)


def rest_kernel(
    out_places, back_places, held_ref, second_ref, left_ref, right_ref, momentum_ref, step_ref,
    new_left_ref, new_right_ref, new_second_ref, new_momentum_ref,
    held_here, second_here, left_here, right_here, momentum_here, step_here, high_ref, low_ref,
    sems, store_sem,
):
    peers, slots, piece_rows, block_size = held_ref.shape

    def load(slot):
        pairs = (
            (left_ref.at[slot], left_here.at[slot]),
            (right_ref.at[slot], right_here.at[slot]),
            (second_ref.at[slot], second_here.at[slot]),
            (momentum_ref.at[slot], momentum_here.at[slot]),
            (step_ref.at[:, slot], step_here.at[:, slot]),
            (held_ref.at[:, slot], held_here.at[:, slot]),
        )[::-1]
        return [started(*pair, sems.at[slot, k]) for k, pair in enumerate(pairs)]

    scale = 0.1 / block_size
    half = block_size // 2
    loads = [load(0)]
    for slot in range(slots):
        loads[slot][0].wait()
        for peer in range(peers):
            rows = rows_of(out_places[peer], piece_rows)
            held = held_here[peer, slot]
            high = held.astype(BF16)
            high_ref[slot, rows, :] = high
            low_ref[slot, rows, :] = (held - high.astype(F32)).astype(BF16)
        for k, (here, ref) in enumerate(
            ((left_here, new_left_ref), (right_here, new_right_ref))
        ):
            product = functools.partial(
                lax.dot_general,
                dimension_numbers=(((1 - k,), (1 - k,)), ((), ())),
                preferred_element_type=F32,
            )
            loads[slot][5 - k].wait()
            for part in range(2):
                cut = slice(part * half, (part + 1) * half)
                at = (slot, cut, slice(None)) if k == 0 else (slot, slice(None), cut)
                gram = (
                    product(high_ref[at], low_ref[slot])
                    + product(low_ref[at], high_ref[slot])
                    + product(high_ref[at], high_ref[slot])
                )
                here[slot, cut, :] = 0.9 * here[slot, cut, :] + scale * gram
            started(here.at[slot], ref.at[slot], store_sem)
        if slot + 1 < slots:
            loads.append(load(slot + 1))
        for pending in loads[slot][1:4]:
            pending.wait()
        for peer in range(peers):
            rows = rows_of(out_places[peer], piece_rows)
            held = held_here[peer, slot]
            second_here[slot, rows, :] = 0.99 * second_here[slot, rows, :] + 0.01 * held * held
            rows = rows_of(back_places[peer], piece_rows)
            momentum_here[slot, rows, :] = (
                0.9 * momentum_here[slot, rows, :] - step_here[peer, slot]
            ) * (1.0 / 1.9)
        started(second_here.at[slot], new_second_ref.at[slot], store_sem)
        started(momentum_here.at[slot], new_momentum_ref.at[slot], store_sem)
    for here in (left_here, right_here, second_here, momentum_here):
        wait_all(here, store_sem)


def body(grad, owner_order, left_stat, right_stat, left_root, right_root, momentum, second):
    slots, block_size = left_stat.shape[0], left_stat.shape[1]
    peers, ranks = lax.axis_size(TENSOR), lax.axis_size(DP + TENSOR)
    out_places, back_places = places_of(OUT_ORDER), places_of(BACK_ORDER)
    piece_rows = block_size // peers
    pair = (peers, slots, piece_rows, block_size)
    blocks = (slots, block_size, block_size)
    hbm = lambda shape: pltpu.HBM(shape, F32)
    vmem = lambda shape, dtype=F32: pltpu.VMEM(shape, dtype)
    exchange = functools.partial(lax.all_to_all, split_axis=0, concat_axis=0, tiled=True)
    order = in_hbm(owner_order)

    outgoing = pl.pallas_call(
        functools.partial(pack_kernel, out_places),
        out_shape=vmem(pair),
        in_specs=[ANY, ANY],
        out_specs=VMEM,
        scratch_shapes=[
            vmem(grad.shape), pltpu.SMEM(owner_order.shape, jnp.int32),
            pltpu.SMEM((peers * slots,), jnp.int32), DMA((2 * CHUNKS,)), DMA,
        ],
        compiler_params=params(8),
        name="pack",
    )(order, in_hbm(grad))
    arrived = exchange(outgoing, OUT_ORDER)

    shampoo, held, sums = pl.pallas_call(
        functools.partial(mid_kernel, out_places),
        out_shape=(vmem(pair), hbm(pair), jax.ShapeDtypeStruct((ranks, 2, 128), F32)),
        in_specs=[VMEM] * 4,
        out_specs=(VMEM, ANY, VMEM),
        scratch_shapes=[vmem(blocks, BF16), vmem(blocks, BF16), DMA],
        compiler_params=params(16),
        name="mid",
    )(in_vmem(arrived), in_vmem(second), in_vmem(left_root), in_vmem(right_root))
    sums = exchange(sums, (DP + TENSOR)[::-1])

    step = pl.pallas_call(
        functools.partial(step_kernel, back_places),
        out_shape=hbm(pair),
        in_specs=[VMEM] * 3,
        out_specs=ANY,
        scratch_shapes=[vmem(pair), DMA],
        compiler_params=params(8),
        name="step",
    )(sums, in_vmem(shampoo), in_vmem(momentum))
    returned = exchange(step, BACK_ORDER)

    new_left, new_right, new_second, new_momentum = pl.pallas_call(
        functools.partial(rest_kernel, out_places, back_places),
        out_shape=(hbm(blocks),) * 4,
        in_specs=[ANY] * 6,
        out_specs=(ANY,) * 4,
        scratch_shapes=[vmem(pair)] + [vmem(blocks)] * 4 + [vmem(pair)]
        + [vmem(blocks, BF16)] * 2 + [DMA((slots, 6)), DMA],
        compiler_params=params(24),
        cost_estimate=pl.CostEstimate(
            flops=slots * 12 * block_size**3, bytes_accessed=18 * MIB, transcendentals=0
        ),
        name="rest",
    )(
        in_hbm(held), in_hbm(second), in_hbm(left_stat), in_hbm(right_stat),
        in_hbm(momentum), in_hbm(step),
    )

    update = pl.pallas_call(
        functools.partial(unpack_kernel, back_places),
        out_shape=hbm(grad.shape),
        in_specs=[pl.BlockSpec(memory_space=pltpu.SMEM), VMEM],
        out_specs=ANY,
        scratch_shapes=[DMA],
        compiler_params=params(8),
        name="unpack",
    )(order, in_vmem(returned))
    return (new_left, new_right, new_momentum, new_second, update)


def solution(mesh):
    names, sizes = zip(*FINE)
    fine = jax.sharding.Mesh(mesh.devices.reshape(sizes), names)
    owned = P(DP + TENSOR, None, None)
    return jax.shard_map(
        body,
        mesh=fine,
        in_specs=(P(TENSOR, DP), P(DP, None)) + (owned,) * 6,
        out_specs=(owned,) * 4 + (P(TENSOR, DP),),
        check_vma=False,
    )
```

```python
import functools

import jax
import jax.numpy as jnp
import numpy as np
from jax import lax
from jax.experimental import pallas as pl
from jax.experimental.pallas import tpu as pltpu
from jax.sharding import PartitionSpec as P

ANY = pl.BlockSpec(memory_space=pl.ANY)
VMEM = pl.BlockSpec(memory_space=pltpu.VMEM)
DMA = pltpu.SemaphoreType.DMA
MIB = 1 << 20
F32 = jnp.float32
BF16 = jnp.bfloat16
CHUNKS = 4


FINE = (("z", 4), ("yh", 2), ("xh", 2), ("xl", 2), ("yl", 2), ("core", 2))
DP, TENSOR = ("z", "yh"), ("xh", "xl", "yl", "core")
OUT_ORDER, BACK_ORDER = ("xl", "xh", "yl", "core"), ("yl", "xl", "xh", "core")


def places_of(order):
    sizes = dict(FINE)
    places = []
    for at in np.ndindex(*(sizes[axis] for axis in order)):
        where = dict(zip(order, at))
        place = 0
        for axis in TENSOR:
            place = place * sizes[axis] + where[axis]
        places.append(place)
    return places


def in_vmem(x):
    return pltpu.with_memory_space_constraint(x, pltpu.VMEM)


def in_hbm(x):
    return pltpu.with_memory_space_constraint(x, pltpu.HBM)


def params(mib):
    return pltpu.CompilerParams(vmem_limit_bytes=mib * MIB)


def copy(source, target, sem):
    return pltpu.make_async_copy(source, target, sem)


def started(source, target, sem):
    moved = copy(source, target, sem)
    moved.start()
    return moved


def wait_all(ref, sem):
    copy(ref, ref, sem).wait()


def piece_of(ref, block, piece_rows, block_size):
    col_blocks = ref.shape[1] // block_size
    row = pl.multiple_of((block // col_blocks) * piece_rows, piece_rows)
    col = pl.multiple_of((block % col_blocks) * block_size, block_size)
    return ref.at[pl.ds(row, piece_rows), pl.ds(col, block_size)]


def rows_of(peer, piece_rows):
    return slice(peer * piece_rows, (peer + 1) * piece_rows)


def pack_kernel(
    places, order_ref, grad_ref, out_ref, here_ref, order_here, index_ref, sems, order_sem
):
    peers, slots, piece_rows, block_size = out_ref.shape
    table = started(order_ref, order_here, order_sem)
    col_blocks = grad_ref.shape[1] // block_size
    chunk_rows = grad_ref.shape[0] // sems.shape[0]
    loads = []
    for chunk in range(sems.shape[0]):
        rows = pl.ds(chunk * chunk_rows, chunk_rows)
        loads.append(started(grad_ref.at[rows], here_ref.at[rows], sems.at[chunk]))
    table.wait()
    for peer in range(peers):
        for slot in range(slots):
            index_ref[order_here[0, places[peer] * slots + slot]] = peer * slots + slot
    for chunk, load in enumerate(loads):
        load.wait()
        for row in range(chunk * chunk_rows, (chunk + 1) * chunk_rows, piece_rows):
            for column in range(col_blocks):
                at = index_ref[row // piece_rows * col_blocks + column]
                out_ref[at // slots, at % slots] = here_ref[
                    row : row + piece_rows, column * block_size : (column + 1) * block_size
                ]


def unpack_kernel(places, order_ref, moved_ref, out_ref, sem):
    peers, slots, piece_rows, block_size = moved_ref.shape
    for peer in range(peers):
        for slot in range(slots):
            block = order_ref[0, places[peer] * slots + slot]
            started(
                moved_ref.at[peer, slot], piece_of(out_ref, block, piece_rows, block_size), sem
            )
    wait_all(moved_ref, sem)


def sum_rows(x):
    return jnp.sum(x.reshape(-1, 8, x.shape[-1]), axis=0)


def mid_kernel(
    places, arrived_ref, second_ref, left_ref, right_ref, shampoo_ref, held_ref, sums_ref,
    low_ref, applied_ref, sem,
):
    peers, slots, piece_rows, block_size = arrived_ref.shape
    kept = started(arrived_ref, held_ref, sem)
    row_order = sorted(range(peers), key=lambda peer: places[peer])

    adam_sq = jnp.zeros((8, block_size), F32)
    shampoo_sq = jnp.zeros((8, block_size), F32)
    for slot in range(slots):
        for peer in row_order:
            rows = rows_of(places[peer], piece_rows)
            held = arrived_ref[peer, slot]
            low_ref[slot, rows, :] = held.astype(BF16)
            new_second = 0.99 * second_ref[slot, rows, :] + 0.01 * held * held
            adam = held * pl.reciprocal(jnp.sqrt(new_second) + 1e-08)
            adam_sq += sum_rows(adam * adam)
    for slot in range(slots):
        applied_ref[slot] = jnp.dot(
            left_ref[slot], low_ref[slot], preferred_element_type=F32
        ).astype(BF16)
    for slot in range(slots):
        shampoo = jnp.dot(applied_ref[slot], right_ref[slot], preferred_element_type=F32)
        shampoo_ref[:, slot] = shampoo.reshape(peers, piece_rows, block_size)
        shampoo_sq += sum_rows(shampoo * shampoo)
    first = lax.broadcasted_iota(jnp.int32, (2, 128), 0) == 0
    sums = jnp.where(first, jnp.sum(adam_sq), jnp.sum(shampoo_sq))
    sums_ref[...] = jnp.broadcast_to(sums[None], sums_ref.shape)
    kept.wait()


def graft_of(sums_ref):
    root = jnp.sqrt(jnp.sum(sums_ref[...], axis=0))
    return root[0:1, 0:1] / (root[1:2, 0:1] + 1e-06)


def step_kernel(places, sums_ref, shampoo_ref, momentum_ref, step_ref, here_ref, sem):
    peers, slots, piece_rows, block_size = shampoo_ref.shape
    graft = graft_of(sums_ref)
    count = peers // (2 * CHUNKS)
    for peer in range(peers):
        rows = rows_of(places[peer], piece_rows)
        for slot in range(slots):
            scaled = graft * shampoo_ref[places[peer], slot]
            new_momentum = 0.9 * momentum_ref[slot, rows, :] + scaled
            here_ref[peer, slot] = -(0.9 * new_momentum + scaled)
        if peer % count == count - 1:
            part = pl.ds(peer - count + 1, count)
            started(here_ref.at[part], step_ref.at[part], sem)
    wait_all(here_ref, sem)


def rest_kernel(
    out_places, back_places, held_ref, second_ref, left_ref, right_ref, momentum_ref, step_ref,
    new_left_ref, new_right_ref, new_second_ref, new_momentum_ref,
    held_here, second_here, left_here, right_here, momentum_here, step_here, high_ref, low_ref,
    sems, store_sem,
):
    peers, slots, piece_rows, block_size = held_ref.shape

    def load(slot):
        pairs = (
            (left_ref.at[slot], left_here.at[slot]),
            (right_ref.at[slot], right_here.at[slot]),
            (second_ref.at[slot], second_here.at[slot]),
            (momentum_ref.at[slot], momentum_here.at[slot]),
            (step_ref.at[:, slot], step_here.at[:, slot]),
            (held_ref.at[:, slot], held_here.at[:, slot]),
        )[::-1]
        return [started(*pair, sems.at[slot, k]) for k, pair in enumerate(pairs)]

    scale = 0.1 / block_size
    half = block_size // 2
    loads = [load(0)]
    for slot in range(slots):
        loads[slot][0].wait()
        for peer in range(peers):
            rows = rows_of(out_places[peer], piece_rows)
            held = held_here[peer, slot]
            high = held.astype(BF16)
            high_ref[slot, rows, :] = high
            low_ref[slot, rows, :] = (held - high.astype(F32)).astype(BF16)
        for k, (here, ref) in enumerate(
            ((left_here, new_left_ref), (right_here, new_right_ref))
        ):
            product = functools.partial(
                lax.dot_general,
                dimension_numbers=(((1 - k,), (1 - k,)), ((), ())),
                preferred_element_type=F32,
            )
            loads[slot][5 - k].wait()
            for part in range(2):
                cut = slice(part * half, (part + 1) * half)
                at = (slot, cut, slice(None)) if k == 0 else (slot, slice(None), cut)
                gram = (
                    product(high_ref[at], low_ref[slot])
                    + product(low_ref[at], high_ref[slot])
                    + product(high_ref[at], high_ref[slot])
                )
                here[slot, cut, :] = 0.9 * here[slot, cut, :] + scale * gram
            started(here.at[slot], ref.at[slot], store_sem)
        if slot + 1 < slots:
            loads.append(load(slot + 1))
        for pending in loads[slot][1:4]:
            pending.wait()
        for peer in range(peers):
            rows = rows_of(out_places[peer], piece_rows)
            held = held_here[peer, slot]
            second_here[slot, rows, :] = 0.99 * second_here[slot, rows, :] + 0.01 * held * held
            rows = rows_of(back_places[peer], piece_rows)
            momentum_here[slot, rows, :] = (
                0.9 * momentum_here[slot, rows, :] - step_here[peer, slot]
            ) * (1.0 / 1.9)
        started(second_here.at[slot], new_second_ref.at[slot], store_sem)
        started(momentum_here.at[slot], new_momentum_ref.at[slot], store_sem)
    for here in (left_here, right_here, second_here, momentum_here):
        wait_all(here, store_sem)


def body(grad, owner_order, left_stat, right_stat, left_root, right_root, momentum, second):
    slots, block_size = left_stat.shape[0], left_stat.shape[1]
    peers, ranks = lax.axis_size(TENSOR), lax.axis_size(DP + TENSOR)
    out_places, back_places = places_of(OUT_ORDER), places_of(BACK_ORDER)
    piece_rows = block_size // peers
    pair = (peers, slots, piece_rows, block_size)
    blocks = (slots, block_size, block_size)
    hbm = lambda shape: pltpu.HBM(shape, F32)
    vmem = lambda shape, dtype=F32: pltpu.VMEM(shape, dtype)
    exchange = functools.partial(lax.all_to_all, split_axis=0, concat_axis=0, tiled=True)
    order = in_hbm(owner_order)

    outgoing = pl.pallas_call(
        functools.partial(pack_kernel, out_places),
        out_shape=vmem(pair),
        in_specs=[ANY, ANY],
        out_specs=VMEM,
        scratch_shapes=[
            vmem(grad.shape), pltpu.SMEM(owner_order.shape, jnp.int32),
            pltpu.SMEM((peers * slots,), jnp.int32), DMA((2 * CHUNKS,)), DMA,
        ],
        compiler_params=params(8),
        name="pack",
    )(order, in_hbm(grad))
    arrived = exchange(outgoing, OUT_ORDER)

    shampoo, held, sums = pl.pallas_call(
        functools.partial(mid_kernel, out_places),
        out_shape=(vmem(pair), hbm(pair), jax.ShapeDtypeStruct((ranks, 2, 128), F32)),
        in_specs=[VMEM] * 4,
        out_specs=(VMEM, ANY, VMEM),
        scratch_shapes=[vmem(blocks, BF16), vmem(blocks, BF16), DMA],
        compiler_params=params(16),
        name="mid",
    )(in_vmem(arrived), in_vmem(second), in_vmem(left_root), in_vmem(right_root))
    sums = exchange(sums, (DP + TENSOR)[::-1])

    step = pl.pallas_call(
        functools.partial(step_kernel, back_places),
        out_shape=hbm(pair),
        in_specs=[VMEM] * 3,
        out_specs=ANY,
        scratch_shapes=[vmem(pair), DMA],
        compiler_params=params(8),
        name="step",
    )(sums, in_vmem(shampoo), in_vmem(momentum))
    returned = exchange(step, BACK_ORDER)

    new_left, new_right, new_second, new_momentum = pl.pallas_call(
        functools.partial(rest_kernel, out_places, back_places),
        out_shape=(hbm(blocks),) * 4,
        in_specs=[ANY] * 6,
        out_specs=(ANY,) * 4,
        scratch_shapes=[vmem(pair)] + [vmem(blocks)] * 4 + [vmem(pair)]
        + [vmem(blocks, BF16)] * 2 + [DMA((slots, 6)), DMA],
        compiler_params=params(24),
        cost_estimate=pl.CostEstimate(
            flops=slots * 12 * block_size**3, bytes_accessed=18 * MIB, transcendentals=0
        ),
        name="rest",
    )(
        in_hbm(held), in_hbm(second), in_hbm(left_stat), in_hbm(right_stat),
        in_hbm(momentum), in_hbm(step),
    )

    update = pl.pallas_call(
        functools.partial(unpack_kernel, back_places),
        out_shape=hbm(grad.shape),
        in_specs=[pl.BlockSpec(memory_space=pltpu.SMEM), VMEM],
        out_specs=ANY,
        scratch_shapes=[DMA],
        compiler_params=params(8),
        name="unpack",
    )(order, in_vmem(returned))
    return (new_left, new_right, new_momentum, new_second, update)


def solution(mesh):
    names, sizes = zip(*FINE)
    fine = jax.sharding.Mesh(mesh.devices.reshape(sizes), names)
    owned = P(DP + TENSOR, None, None)
    return jax.shard_map(
        body,
        mesh=fine,
        in_specs=(P(TENSOR, DP), P(DP, None)) + (owned,) * 6,
        out_specs=(owned,) * 4 + (P(TENSOR, DP),),
        check_vma=False,
    )
```

```python
import functools

import jax
import jax.numpy as jnp
import numpy as np
from jax import lax
from jax.experimental import pallas as pl
from jax.experimental.pallas import tpu as pltpu
from jax.sharding import PartitionSpec as P

ANY = pl.BlockSpec(memory_space=pl.ANY)
VMEM = pl.BlockSpec(memory_space=pltpu.VMEM)
DMA = pltpu.SemaphoreType.DMA
MIB = 1 << 20
F32 = jnp.float32
BF16 = jnp.bfloat16
CHUNKS = 4


FINE = (("z", 4), ("yh", 2), ("x", 4), ("yl", 2), ("core", 2))
DP, TENSOR = ("z", "yh"), ("x", "yl", "core")
OUT_ORDER, BACK_ORDER = TENSOR, TENSOR


def places_of(order):
    sizes = dict(FINE)
    places = []
    for at in np.ndindex(*(sizes[axis] for axis in order)):
        where = dict(zip(order, at))
        place = 0
        for axis in TENSOR:
            place = place * sizes[axis] + where[axis]
        places.append(place)
    return places


def in_vmem(x):
    return pltpu.with_memory_space_constraint(x, pltpu.VMEM)


def in_hbm(x):
    return pltpu.with_memory_space_constraint(x, pltpu.HBM)


def params(mib):
    return pltpu.CompilerParams(vmem_limit_bytes=mib * MIB)


def copy(source, target, sem):
    return pltpu.make_async_copy(source, target, sem)


def started(source, target, sem):
    moved = copy(source, target, sem)
    moved.start()
    return moved


def wait_all(ref, sem):
    copy(ref, ref, sem).wait()


def piece_of(ref, block, piece_rows, block_size):
    col_blocks = ref.shape[1] // block_size
    row = pl.multiple_of((block // col_blocks) * piece_rows, piece_rows)
    col = pl.multiple_of((block % col_blocks) * block_size, block_size)
    return ref.at[pl.ds(row, piece_rows), pl.ds(col, block_size)]


def rows_of(peer, piece_rows):
    return slice(peer * piece_rows, (peer + 1) * piece_rows)


def pack_kernel(
    places, order_ref, grad_ref, out_ref, here_ref, order_here, index_ref, sems, order_sem
):
    peers, slots, piece_rows, block_size = out_ref.shape
    table = started(order_ref, order_here, order_sem)
    col_blocks = grad_ref.shape[1] // block_size
    chunk_rows = grad_ref.shape[0] // sems.shape[0]
    loads = []
    for chunk in range(sems.shape[0]):
        rows = pl.ds(chunk * chunk_rows, chunk_rows)
        loads.append(started(grad_ref.at[rows], here_ref.at[rows], sems.at[chunk]))
    table.wait()
    for peer in range(peers):
        for slot in range(slots):
            index_ref[order_here[0, places[peer] * slots + slot]] = peer * slots + slot
    for chunk, load in enumerate(loads):
        load.wait()
        for row in range(chunk * chunk_rows, (chunk + 1) * chunk_rows, piece_rows):
            for column in range(col_blocks):
                at = index_ref[row // piece_rows * col_blocks + column]
                out_ref[at // slots, at % slots] = here_ref[
                    row : row + piece_rows, column * block_size : (column + 1) * block_size
                ]


def unpack_kernel(places, order_ref, moved_ref, out_ref, sem):
    peers, slots, piece_rows, block_size = moved_ref.shape
    for peer in range(peers):
        for slot in range(slots):
            block = order_ref[0, places[peer] * slots + slot]
            started(
                moved_ref.at[peer, slot], piece_of(out_ref, block, piece_rows, block_size), sem
            )
    wait_all(moved_ref, sem)


def sum_rows(x):
    return jnp.sum(x.reshape(-1, 8, x.shape[-1]), axis=0)


def mid_kernel(
    places, arrived_ref, second_ref, left_ref, right_ref, shampoo_ref, held_ref, sums_ref,
    low_ref, applied_ref, sem,
):
    peers, slots, piece_rows, block_size = arrived_ref.shape
    kept = started(arrived_ref, held_ref, sem)
    row_order = sorted(range(peers), key=lambda peer: places[peer])

    adam_sq = jnp.zeros((8, block_size), F32)
    shampoo_sq = jnp.zeros((8, block_size), F32)
    for slot in range(slots):
        for peer in row_order:
            rows = rows_of(places[peer], piece_rows)
            held = arrived_ref[peer, slot]
            low_ref[slot, rows, :] = held.astype(BF16)
            new_second = 0.99 * second_ref[slot, rows, :] + 0.01 * held * held
            adam = held * pl.reciprocal(jnp.sqrt(new_second) + 1e-08)
            adam_sq += sum_rows(adam * adam)
        applied_ref[slot] = jnp.dot(
            left_ref[slot], low_ref[slot], preferred_element_type=F32
        ).astype(BF16)
    for slot in range(slots):
        shampoo = jnp.dot(applied_ref[slot], right_ref[slot], preferred_element_type=F32)
        shampoo_ref[:, slot] = shampoo.reshape(peers, piece_rows, block_size)
        shampoo_sq += sum_rows(shampoo * shampoo)
    first = lax.broadcasted_iota(jnp.int32, (2, 128), 0) == 0
    sums = jnp.where(first, jnp.sum(adam_sq), jnp.sum(shampoo_sq))
    sums_ref[...] = jnp.broadcast_to(sums[None], sums_ref.shape)
    kept.wait()


def graft_of(sums_ref):
    root = jnp.sqrt(jnp.sum(sums_ref[...], axis=0))
    return root[0:1, 0:1] / (root[1:2, 0:1] + 1e-06)


def step_kernel(places, sums_ref, shampoo_ref, momentum_ref, step_ref, here_ref, sem):
    peers, slots, piece_rows, block_size = shampoo_ref.shape
    graft = graft_of(sums_ref)
    count = peers // (2 * CHUNKS)
    for peer in range(peers):
        rows = rows_of(places[peer], piece_rows)
        for slot in range(slots):
            scaled = graft * shampoo_ref[places[peer], slot]
            new_momentum = 0.9 * momentum_ref[slot, rows, :] + scaled
            here_ref[peer, slot] = -(0.9 * new_momentum + scaled)
        if peer % count == count - 1:
            part = pl.ds(peer - count + 1, count)
            started(here_ref.at[part], step_ref.at[part], sem)
    wait_all(here_ref, sem)


def rest_kernel(
    out_places, back_places, held_ref, second_ref, left_ref, right_ref, momentum_ref, step_ref,
    new_left_ref, new_right_ref, new_second_ref, new_momentum_ref,
    held_here, second_here, left_here, right_here, momentum_here, step_here, high_ref, low_ref,
    sems, store_sem,
):
    peers, slots, piece_rows, block_size = held_ref.shape

    def load(slot):
        pairs = (
            (left_ref.at[slot], left_here.at[slot]),
            (right_ref.at[slot], right_here.at[slot]),
            (second_ref.at[slot], second_here.at[slot]),
            (momentum_ref.at[slot], momentum_here.at[slot]),
            (step_ref.at[:, slot], step_here.at[:, slot]),
            (held_ref.at[:, slot], held_here.at[:, slot]),
        )[::-1]
        return [started(*pair, sems.at[slot, k]) for k, pair in enumerate(pairs)]

    scale = 0.1 / block_size
    half = block_size // 2
    loads = [load(0)]
    for slot in range(slots):
        loads[slot][0].wait()
        for peer in range(peers):
            rows = rows_of(out_places[peer], piece_rows)
            held = held_here[peer, slot]
            high = held.astype(BF16)
            high_ref[slot, rows, :] = high
            low_ref[slot, rows, :] = (held - high.astype(F32)).astype(BF16)
        for k, (here, ref) in enumerate(
            ((left_here, new_left_ref), (right_here, new_right_ref))
        ):
            product = functools.partial(
                lax.dot_general,
                dimension_numbers=(((1 - k,), (1 - k,)), ((), ())),
                preferred_element_type=F32,
            )
            loads[slot][5 - k].wait()
            for part in range(2):
                cut = slice(part * half, (part + 1) * half)
                at = (slot, cut, slice(None)) if k == 0 else (slot, slice(None), cut)
                gram = (
                    product(high_ref[at], low_ref[slot])
                    + product(low_ref[at], high_ref[slot])
                    + product(high_ref[at], high_ref[slot])
                )
                here[slot, cut, :] = 0.9 * here[slot, cut, :] + scale * gram
            started(here.at[slot], ref.at[slot], store_sem)
        if slot + 1 < slots:
            loads.append(load(slot + 1))
        for pending in loads[slot][1:4]:
            pending.wait()
        for peer in range(peers):
            rows = rows_of(out_places[peer], piece_rows)
            held = held_here[peer, slot]
            second_here[slot, rows, :] = 0.99 * second_here[slot, rows, :] + 0.01 * held * held
            rows = rows_of(back_places[peer], piece_rows)
            momentum_here[slot, rows, :] = (
                0.9 * momentum_here[slot, rows, :] - step_here[peer, slot]
            ) * (1.0 / 1.9)
        started(second_here.at[slot], new_second_ref.at[slot], store_sem)
        started(momentum_here.at[slot], new_momentum_ref.at[slot], store_sem)
    for here in (left_here, right_here, second_here, momentum_here):
        wait_all(here, store_sem)


def body(grad, owner_order, left_stat, right_stat, left_root, right_root, momentum, second):
    slots, block_size = left_stat.shape[0], left_stat.shape[1]
    peers, ranks = lax.axis_size(TENSOR), lax.axis_size(DP + TENSOR)
    out_places, back_places = places_of(OUT_ORDER), places_of(BACK_ORDER)
    piece_rows = block_size // peers
    pair = (peers, slots, piece_rows, block_size)
    blocks = (slots, block_size, block_size)
    hbm = lambda shape: pltpu.HBM(shape, F32)
    vmem = lambda shape, dtype=F32: pltpu.VMEM(shape, dtype)
    exchange = functools.partial(lax.all_to_all, split_axis=0, concat_axis=0, tiled=True)
    order = in_hbm(owner_order)

    outgoing = pl.pallas_call(
        functools.partial(pack_kernel, out_places),
        out_shape=vmem(pair),
        in_specs=[ANY, ANY],
        out_specs=VMEM,
        scratch_shapes=[
            vmem(grad.shape), pltpu.SMEM(owner_order.shape, jnp.int32),
            pltpu.SMEM((peers * slots,), jnp.int32), DMA((2 * CHUNKS,)), DMA,
        ],
        compiler_params=params(8),
        name="pack",
    )(order, in_hbm(grad))
    arrived = exchange(outgoing, OUT_ORDER)

    shampoo, held, sums = pl.pallas_call(
        functools.partial(mid_kernel, out_places),
        out_shape=(vmem(pair), hbm(pair), jax.ShapeDtypeStruct((ranks, 2, 128), F32)),
        in_specs=[VMEM] * 4,
        out_specs=(VMEM, ANY, VMEM),
        scratch_shapes=[vmem(blocks, BF16), vmem(blocks, BF16), DMA],
        compiler_params=params(16),
        name="mid",
    )(in_vmem(arrived), in_vmem(second), in_vmem(left_root), in_vmem(right_root))
    sums = exchange(sums, (DP + TENSOR)[::-1])

    step = pl.pallas_call(
        functools.partial(step_kernel, back_places),
        out_shape=hbm(pair),
        in_specs=[VMEM] * 3,
        out_specs=ANY,
        scratch_shapes=[vmem(pair), DMA],
        compiler_params=params(8),
        name="step",
    )(sums, in_vmem(shampoo), in_vmem(momentum))
    returned = exchange(step, BACK_ORDER)

    new_left, new_right, new_second, new_momentum = pl.pallas_call(
        functools.partial(rest_kernel, out_places, back_places),
        out_shape=(hbm(blocks),) * 4,
        in_specs=[ANY] * 6,
        out_specs=(ANY,) * 4,
        scratch_shapes=[vmem(pair)] + [vmem(blocks)] * 4 + [vmem(pair)]
        + [vmem(blocks, BF16)] * 2 + [DMA((slots, 6)), DMA],
        compiler_params=params(24),
        cost_estimate=pl.CostEstimate(
            flops=slots * 12 * block_size**3, bytes_accessed=18 * MIB, transcendentals=0
        ),
        name="rest",
    )(
        in_hbm(held), in_hbm(second), in_hbm(left_stat), in_hbm(right_stat),
        in_hbm(momentum), in_hbm(step),
    )

    update = pl.pallas_call(
        functools.partial(unpack_kernel, back_places),
        out_shape=hbm(grad.shape),
        in_specs=[pl.BlockSpec(memory_space=pltpu.SMEM), VMEM],
        out_specs=ANY,
        scratch_shapes=[DMA],
        compiler_params=params(8),
        name="unpack",
    )(order, in_vmem(returned))
    return (new_left, new_right, new_momentum, new_second, update)


def solution(mesh):
    names, sizes = zip(*FINE)
    fine = jax.sharding.Mesh(mesh.devices.reshape(sizes), names)
    owned = P(DP + TENSOR, None, None)
    return jax.shard_map(
        body,
        mesh=fine,
        in_specs=(P(TENSOR, DP), P(DP, None)) + (owned,) * 6,
        out_specs=(owned,) * 4 + (P(TENSOR, DP),),
        check_vma=False,
    )
```

```python
import functools

import jax
import jax.numpy as jnp
import numpy as np
from jax import lax
from jax.experimental import pallas as pl
from jax.experimental.pallas import tpu as pltpu
from jax.sharding import PartitionSpec as P

ANY = pl.BlockSpec(memory_space=pl.ANY)
VMEM = pl.BlockSpec(memory_space=pltpu.VMEM)
DMA = pltpu.SemaphoreType.DMA
MIB = 1 << 20
F32 = jnp.float32
BF16 = jnp.bfloat16
CHUNKS = 4


FINE = (("z", 4), ("yh", 2), ("x", 4), ("yl", 2), ("core", 2))
DP, TENSOR = ("z", "yh"), ("x", "yl", "core")
OUT_ORDER, BACK_ORDER = TENSOR, TENSOR


def places_of(order):
    sizes = dict(FINE)
    places = []
    for at in np.ndindex(*(sizes[axis] for axis in order)):
        where = dict(zip(order, at))
        place = 0
        for axis in TENSOR:
            place = place * sizes[axis] + where[axis]
        places.append(place)
    return places


def in_vmem(x):
    return pltpu.with_memory_space_constraint(x, pltpu.VMEM)


def in_hbm(x):
    return pltpu.with_memory_space_constraint(x, pltpu.HBM)


def params(mib):
    return pltpu.CompilerParams(vmem_limit_bytes=mib * MIB)


def copy(source, target, sem):
    return pltpu.make_async_copy(source, target, sem)


def started(source, target, sem):
    moved = copy(source, target, sem)
    moved.start()
    return moved


def wait_all(ref, sem):
    copy(ref, ref, sem).wait()


def piece_of(ref, block, piece_rows, block_size):
    col_blocks = ref.shape[1] // block_size
    row = pl.multiple_of((block // col_blocks) * piece_rows, piece_rows)
    col = pl.multiple_of((block % col_blocks) * block_size, block_size)
    return ref.at[pl.ds(row, piece_rows), pl.ds(col, block_size)]


def rows_of(peer, piece_rows):
    return slice(peer * piece_rows, (peer + 1) * piece_rows)


def pack_kernel(
    places, order_ref, grad_ref, out_ref, order_here, here_ref, index_ref, sems, order_sem
):
    peers, slots, piece_rows, block_size = out_ref.shape
    table = started(order_ref, order_here, order_sem)
    col_blocks = grad_ref.shape[1] // block_size
    chunk_rows = grad_ref.shape[0] // sems.shape[0]
    loads = []
    for chunk in range(sems.shape[0]):
        rows = pl.ds(chunk * chunk_rows, chunk_rows)
        loads.append(started(grad_ref.at[rows], here_ref.at[rows], sems.at[chunk]))
    table.wait()
    for peer in range(peers):
        for slot in range(slots):
            index_ref[order_here[0, places[peer] * slots + slot]] = peer * slots + slot
    for chunk, load in enumerate(loads):
        load.wait()
        for row in range(chunk * chunk_rows, (chunk + 1) * chunk_rows, piece_rows):
            for column in range(col_blocks):
                at = index_ref[row // piece_rows * col_blocks + column]
                out_ref[at // slots, at % slots] = here_ref[
                    row : row + piece_rows, column * block_size : (column + 1) * block_size
                ]


def unpack_kernel(places, order_ref, moved_ref, out_ref, sem):
    peers, slots, piece_rows, block_size = moved_ref.shape
    for peer in range(peers):
        for slot in range(slots):
            block = order_ref[0, places[peer] * slots + slot]
            started(
                moved_ref.at[peer, slot], piece_of(out_ref, block, piece_rows, block_size), sem
            )
    wait_all(moved_ref, sem)


def sum_rows(x):
    return jnp.sum(x.reshape(-1, 8, x.shape[-1]), axis=0)


def mid_kernel(
    places, arrived_ref, second_ref, left_ref, right_ref, shampoo_ref, held_ref, sums_ref,
    low_ref, applied_ref, sem,
):
    peers, slots, piece_rows, block_size = arrived_ref.shape
    kept = started(arrived_ref, held_ref, sem)
    row_order = sorted(range(peers), key=lambda peer: places[peer])

    adam_sq = jnp.zeros((8, block_size), F32)
    shampoo_sq = jnp.zeros((8, block_size), F32)
    for slot in range(slots):
        for peer in row_order:
            rows = rows_of(places[peer], piece_rows)
            held = arrived_ref[peer, slot]
            low_ref[slot, rows, :] = held.astype(BF16)
            new_second = 0.99 * second_ref[slot, rows, :] + 0.01 * held * held
            adam = held * pl.reciprocal(jnp.sqrt(new_second) + 1e-08)
            adam_sq += sum_rows(adam * adam)
    for slot in range(slots):
        applied_ref[slot] = jnp.dot(
            left_ref[slot], low_ref[slot], preferred_element_type=F32
        ).astype(BF16)
    for slot in range(slots):
        shampoo = jnp.dot(applied_ref[slot], right_ref[slot], preferred_element_type=F32)
        shampoo_ref[:, slot] = shampoo.reshape(peers, piece_rows, block_size)
        shampoo_sq += sum_rows(shampoo * shampoo)
    first = lax.broadcasted_iota(jnp.int32, (2, 128), 0) == 0
    sums = jnp.where(first, jnp.sum(adam_sq), jnp.sum(shampoo_sq))
    sums_ref[...] = jnp.broadcast_to(sums[None], sums_ref.shape)
    kept.wait()


def graft_of(sums_ref):
    root = jnp.sqrt(jnp.sum(sums_ref[...], axis=0))
    return root[0:1, 0:1] / (root[1:2, 0:1] + 1e-06)


def step_kernel(places, sums_ref, shampoo_ref, momentum_ref, step_ref, here_ref, sem):
    peers, slots, piece_rows, block_size = shampoo_ref.shape
    graft = graft_of(sums_ref)
    count = peers // (2 * CHUNKS)
    for peer in range(peers):
        rows = rows_of(places[peer], piece_rows)
        for slot in range(slots):
            scaled = graft * shampoo_ref[places[peer], slot]
            new_momentum = 0.9 * momentum_ref[slot, rows, :] + scaled
            here_ref[peer, slot] = -(0.9 * new_momentum + scaled)
        if peer % count == count - 1:
            part = pl.ds(peer - count + 1, count)
            started(here_ref.at[part], step_ref.at[part], sem)
    wait_all(here_ref, sem)


def rest_kernel(
    out_places, back_places, held_ref, second_ref, left_ref, right_ref, momentum_ref, step_ref,
    new_left_ref, new_right_ref, new_second_ref, new_momentum_ref,
    held_here, second_here, left_here, right_here, momentum_here, step_here, high_ref, low_ref,
    sems, store_sem,
):
    peers, slots, piece_rows, block_size = held_ref.shape

    def load(slot):
        pairs = (
            (left_ref.at[slot], left_here.at[slot]),
            (right_ref.at[slot], right_here.at[slot]),
            (second_ref.at[slot], second_here.at[slot]),
            (momentum_ref.at[slot], momentum_here.at[slot]),
            (step_ref.at[:, slot], step_here.at[:, slot]),
            (held_ref.at[:, slot], held_here.at[:, slot]),
        )[::-1]
        return [started(*pair, sems.at[slot, k]) for k, pair in enumerate(pairs)]

    scale = 0.1 / block_size
    half = block_size // 2
    loads = [load(0)]
    for slot in range(slots):
        loads[slot][0].wait()
        for peer in range(peers):
            rows = rows_of(out_places[peer], piece_rows)
            held = held_here[peer, slot]
            high = held.astype(BF16)
            high_ref[slot, rows, :] = high
            low_ref[slot, rows, :] = (held - high.astype(F32)).astype(BF16)
        for k, (here, ref) in enumerate(
            ((left_here, new_left_ref), (right_here, new_right_ref))
        ):
            product = functools.partial(
                lax.dot_general,
                dimension_numbers=(((1 - k,), (1 - k,)), ((), ())),
                preferred_element_type=F32,
            )
            loads[slot][5 - k].wait()
            for part in range(2):
                cut = slice(part * half, (part + 1) * half)
                at = (slot, cut, slice(None)) if k == 0 else (slot, slice(None), cut)
                gram = (
                    product(high_ref[at], low_ref[slot])
                    + product(low_ref[at], high_ref[slot])
                    + product(high_ref[at], high_ref[slot])
                )
                here[slot, cut, :] = 0.9 * here[slot, cut, :] + scale * gram
            started(here.at[slot], ref.at[slot], store_sem)
        if slot + 1 < slots:
            loads.append(load(slot + 1))
        for pending in loads[slot][1:4]:
            pending.wait()
        for peer in range(peers):
            rows = rows_of(out_places[peer], piece_rows)
            held = held_here[peer, slot]
            second_here[slot, rows, :] = 0.99 * second_here[slot, rows, :] + 0.01 * held * held
            rows = rows_of(back_places[peer], piece_rows)
            momentum_here[slot, rows, :] = (
                0.9 * momentum_here[slot, rows, :] - step_here[peer, slot]
            ) * (1.0 / 1.9)
        started(second_here.at[slot], new_second_ref.at[slot], store_sem)
        started(momentum_here.at[slot], new_momentum_ref.at[slot], store_sem)
    for here in (left_here, right_here, second_here, momentum_here):
        wait_all(here, store_sem)


def body(grad, owner_order, left_stat, right_stat, left_root, right_root, momentum, second):
    slots, block_size = left_stat.shape[0], left_stat.shape[1]
    peers, ranks = lax.axis_size(TENSOR), lax.axis_size(DP + TENSOR)
    out_places, back_places = places_of(OUT_ORDER), places_of(BACK_ORDER)
    piece_rows = block_size // peers
    pair = (peers, slots, piece_rows, block_size)
    blocks = (slots, block_size, block_size)
    hbm = lambda shape: pltpu.HBM(shape, F32)
    vmem = lambda shape, dtype=F32: pltpu.VMEM(shape, dtype)
    exchange = functools.partial(lax.all_to_all, split_axis=0, concat_axis=0, tiled=True)
    order = in_hbm(owner_order)

    outgoing, table = pl.pallas_call(
        functools.partial(pack_kernel, out_places),
        out_shape=(vmem(pair), pltpu.SMEM(owner_order.shape, jnp.int32)),
        in_specs=[ANY, ANY],
        out_specs=(VMEM, pl.BlockSpec(memory_space=pltpu.SMEM)),
        scratch_shapes=[
            vmem(grad.shape), pltpu.SMEM((peers * slots,), jnp.int32), DMA((2 * CHUNKS,)), DMA,
        ],
        compiler_params=params(8),
        name="pack",
    )(order, in_hbm(grad))
    arrived = exchange(outgoing, OUT_ORDER)

    shampoo, held, sums = pl.pallas_call(
        functools.partial(mid_kernel, out_places),
        out_shape=(vmem(pair), hbm(pair), jax.ShapeDtypeStruct((ranks, 2, 128), F32)),
        in_specs=[VMEM] * 4,
        out_specs=(VMEM, ANY, VMEM),
        scratch_shapes=[vmem(blocks, BF16), vmem(blocks, BF16), DMA],
        compiler_params=params(16),
        name="mid",
    )(in_vmem(arrived), in_vmem(second), in_vmem(left_root), in_vmem(right_root))
    sums = exchange(sums, (DP + TENSOR)[::-1])

    step = pl.pallas_call(
        functools.partial(step_kernel, back_places),
        out_shape=hbm(pair),
        in_specs=[VMEM] * 3,
        out_specs=ANY,
        scratch_shapes=[vmem(pair), DMA],
        compiler_params=params(8),
        name="step",
    )(sums, in_vmem(shampoo), in_vmem(momentum))
    returned = exchange(step, BACK_ORDER)

    new_left, new_right, new_second, new_momentum = pl.pallas_call(
        functools.partial(rest_kernel, out_places, back_places),
        out_shape=(hbm(blocks),) * 4,
        in_specs=[ANY] * 6,
        out_specs=(ANY,) * 4,
        scratch_shapes=[vmem(pair)] + [vmem(blocks)] * 4 + [vmem(pair)]
        + [vmem(blocks, BF16)] * 2 + [DMA((slots, 6)), DMA],
        compiler_params=params(24),
        cost_estimate=pl.CostEstimate(
            flops=slots * 12 * block_size**3, bytes_accessed=18 * MIB, transcendentals=0
        ),
        name="rest",
    )(
        in_hbm(held), in_hbm(second), in_hbm(left_stat), in_hbm(right_stat),
        in_hbm(momentum), in_hbm(step),
    )

    update = pl.pallas_call(
        functools.partial(unpack_kernel, back_places),
        out_shape=hbm(grad.shape),
        in_specs=[pl.BlockSpec(memory_space=pltpu.SMEM), VMEM],
        out_specs=ANY,
        scratch_shapes=[DMA],
        compiler_params=params(8),
        name="unpack",
    )(table, in_vmem(returned))
    return (new_left, new_right, new_momentum, new_second, update)


def solution(mesh):
    names, sizes = zip(*FINE)
    fine = jax.sharding.Mesh(mesh.devices.reshape(sizes), names)
    owned = P(DP + TENSOR, None, None)
    return jax.shard_map(
        body,
        mesh=fine,
        in_specs=(P(TENSOR, DP), P(DP, None)) + (owned,) * 6,
        out_specs=(owned,) * 4 + (P(TENSOR, DP),),
        check_vma=False,
    )
```

```python
import functools

import jax
import jax.numpy as jnp
import numpy as np
from jax import lax
from jax.experimental import pallas as pl
from jax.experimental.pallas import tpu as pltpu
from jax.sharding import PartitionSpec as P

ANY = pl.BlockSpec(memory_space=pl.ANY)
VMEM = pl.BlockSpec(memory_space=pltpu.VMEM)
DMA = pltpu.SemaphoreType.DMA
MIB = 1 << 20
F32 = jnp.float32
BF16 = jnp.bfloat16
CHUNKS = 4


FINE = (("z", 4), ("yh", 2), ("x", 4), ("yl", 2), ("core", 2))
DP, TENSOR = ("z", "yh"), ("x", "yl", "core")
OUT_ORDER, BACK_ORDER = TENSOR, TENSOR


def places_of(order):
    sizes = dict(FINE)
    places = []
    for at in np.ndindex(*(sizes[axis] for axis in order)):
        where = dict(zip(order, at))
        place = 0
        for axis in TENSOR:
            place = place * sizes[axis] + where[axis]
        places.append(place)
    return places


def in_vmem(x):
    return pltpu.with_memory_space_constraint(x, pltpu.VMEM)


def in_hbm(x):
    return pltpu.with_memory_space_constraint(x, pltpu.HBM)


def params(mib):
    return pltpu.CompilerParams(vmem_limit_bytes=mib * MIB)


def copy(source, target, sem):
    return pltpu.make_async_copy(source, target, sem)


def started(source, target, sem):
    moved = copy(source, target, sem)
    moved.start()
    return moved


def wait_all(ref, sem):
    copy(ref, ref, sem).wait()


def piece_of(ref, block, piece_rows, block_size):
    col_blocks = ref.shape[1] // block_size
    row = pl.multiple_of((block // col_blocks) * piece_rows, piece_rows)
    col = pl.multiple_of((block % col_blocks) * block_size, block_size)
    return ref.at[pl.ds(row, piece_rows), pl.ds(col, block_size)]


def rows_of(peer, piece_rows):
    return slice(peer * piece_rows, (peer + 1) * piece_rows)


def pack_kernel(
    places, order_ref, grad_ref, out_ref, order_here, here_ref, index_ref, sems, order_sem
):
    peers, slots, piece_rows, block_size = out_ref.shape
    table = started(order_ref, order_here, order_sem)
    col_blocks = grad_ref.shape[1] // block_size
    chunk_rows = grad_ref.shape[0] // sems.shape[0]
    loads = []
    for chunk in range(sems.shape[0]):
        rows = pl.ds(chunk * chunk_rows, chunk_rows)
        loads.append(started(grad_ref.at[rows], here_ref.at[rows], sems.at[chunk]))
    table.wait()
    for peer in range(peers):
        for slot in range(slots):
            index_ref[order_here[0, places[peer] * slots + slot]] = peer * slots + slot
    for chunk, load in enumerate(loads):
        load.wait()
        for row in range(chunk * chunk_rows, (chunk + 1) * chunk_rows, piece_rows):
            for column in range(col_blocks):
                at = index_ref[row // piece_rows * col_blocks + column]
                out_ref[at // slots, at % slots] = here_ref[
                    row : row + piece_rows, column * block_size : (column + 1) * block_size
                ]


def unpack_kernel(places, order_ref, moved_ref, out_ref, sem):
    peers, slots, piece_rows, block_size = moved_ref.shape
    for peer in range(peers):
        for slot in range(slots):
            block = order_ref[0, places[peer] * slots + slot]
            started(
                moved_ref.at[peer, slot], piece_of(out_ref, block, piece_rows, block_size), sem
            )
    wait_all(moved_ref, sem)


def sum_rows(x):
    return jnp.sum(x.reshape(-1, 8, x.shape[-1]), axis=0)


def mid_kernel(
    places, arrived_ref, second_ref, left_ref, right_ref, shampoo_ref, held_ref, sums_ref,
    low_ref, applied_ref, sem,
):
    peers, slots, piece_rows, block_size = arrived_ref.shape
    kept = started(arrived_ref, held_ref, sem)
    row_order = sorted(range(peers), key=lambda peer: places[peer])

    adam_sq = jnp.zeros((8, block_size), F32)
    shampoo_sq = jnp.zeros((8, block_size), F32)
    for slot in range(slots):
        for peer in row_order:
            rows = rows_of(places[peer], piece_rows)
            held = arrived_ref[peer, slot]
            low_ref[slot, rows, :] = held.astype(BF16)
            new_second = 0.99 * second_ref[slot, rows, :] + 0.01 * held * held
            adam = held * pl.reciprocal(jnp.sqrt(new_second) + 1e-08)
            adam_sq += sum_rows(adam * adam)
    for slot in range(slots):
        applied_ref[slot] = jnp.dot(
            left_ref[slot], low_ref[slot], preferred_element_type=F32
        ).astype(BF16)
    for slot in range(slots):
        shampoo = jnp.dot(applied_ref[slot], right_ref[slot], preferred_element_type=F32)
        shampoo_ref[:, slot] = shampoo.reshape(peers, piece_rows, block_size)
        shampoo_sq += sum_rows(shampoo * shampoo)
    first = lax.broadcasted_iota(jnp.int32, (1, 128), 1) < 64
    sums = jnp.where(first, jnp.sum(adam_sq), jnp.sum(shampoo_sq))
    sums_ref[...] = jnp.broadcast_to(sums[None], sums_ref.shape)
    kept.wait()


def graft_of(sums_ref):
    root = jnp.sqrt(jnp.sum(sums_ref[...], axis=0))
    return root[0:1, 0:1] / (root[0:1, 64:65] + 1e-06)


def step_kernel(places, sums_ref, shampoo_ref, momentum_ref, step_ref, here_ref, sem):
    peers, slots, piece_rows, block_size = shampoo_ref.shape
    graft = graft_of(sums_ref)
    count = peers // (4 * CHUNKS)
    for peer in range(peers):
        rows = rows_of(places[peer], piece_rows)
        for slot in range(slots):
            scaled = graft * shampoo_ref[places[peer], slot]
            new_momentum = 0.9 * momentum_ref[slot, rows, :] + scaled
            here_ref[peer, slot] = -(0.9 * new_momentum + scaled)
        if peer % count == count - 1:
            part = pl.ds(peer - count + 1, count)
            started(here_ref.at[part], step_ref.at[part], sem)
    wait_all(here_ref, sem)


def rest_kernel(
    out_places, back_places, held_ref, second_ref, left_ref, right_ref, momentum_ref, step_ref,
    new_left_ref, new_right_ref, new_second_ref, new_momentum_ref,
    held_here, second_here, left_here, right_here, momentum_here, step_here, high_ref, low_ref,
    sems, store_sem,
):
    peers, slots, piece_rows, block_size = held_ref.shape

    def load(slot):
        pairs = (
            (left_ref.at[slot], left_here.at[slot]),
            (right_ref.at[slot], right_here.at[slot]),
            (second_ref.at[slot], second_here.at[slot]),
            (momentum_ref.at[slot], momentum_here.at[slot]),
            (step_ref.at[:, slot], step_here.at[:, slot]),
            (held_ref.at[:, slot], held_here.at[:, slot]),
        )[::-1]
        return [started(*pair, sems.at[slot, k]) for k, pair in enumerate(pairs)]

    scale = 0.1 / block_size
    half = block_size // 2
    loads = [load(0)]
    for slot in range(slots):
        loads[slot][0].wait()
        for peer in range(peers):
            rows = rows_of(out_places[peer], piece_rows)
            held = held_here[peer, slot]
            high = held.astype(BF16)
            high_ref[slot, rows, :] = high
            low_ref[slot, rows, :] = (held - high.astype(F32)).astype(BF16)
        for k, (here, ref) in enumerate(
            ((left_here, new_left_ref), (right_here, new_right_ref))
        ):
            product = functools.partial(
                lax.dot_general,
                dimension_numbers=(((1 - k,), (1 - k,)), ((), ())),
                preferred_element_type=F32,
            )
            loads[slot][5 - k].wait()
            for part in range(2):
                cut = slice(part * half, (part + 1) * half)
                at = (slot, cut, slice(None)) if k == 0 else (slot, slice(None), cut)
                gram = (
                    product(high_ref[at], low_ref[slot])
                    + product(low_ref[at], high_ref[slot])
                    + product(high_ref[at], high_ref[slot])
                )
                here[slot, cut, :] = 0.9 * here[slot, cut, :] + scale * gram
            started(here.at[slot], ref.at[slot], store_sem)
        if slot + 1 < slots:
            loads.append(load(slot + 1))
        for pending in loads[slot][1:4]:
            pending.wait()
        for peer in range(peers):
            rows = rows_of(out_places[peer], piece_rows)
            held = held_here[peer, slot]
            second_here[slot, rows, :] = 0.99 * second_here[slot, rows, :] + 0.01 * held * held
            rows = rows_of(back_places[peer], piece_rows)
            momentum_here[slot, rows, :] = (
                0.9 * momentum_here[slot, rows, :] - step_here[peer, slot]
            ) * (1.0 / 1.9)
        started(second_here.at[slot], new_second_ref.at[slot], store_sem)
        started(momentum_here.at[slot], new_momentum_ref.at[slot], store_sem)
    for here in (left_here, right_here, second_here, momentum_here):
        wait_all(here, store_sem)


def body(grad, owner_order, left_stat, right_stat, left_root, right_root, momentum, second):
    slots, block_size = left_stat.shape[0], left_stat.shape[1]
    peers, ranks = lax.axis_size(TENSOR), lax.axis_size(DP + TENSOR)
    out_places, back_places = places_of(OUT_ORDER), places_of(BACK_ORDER)
    piece_rows = block_size // peers
    pair = (peers, slots, piece_rows, block_size)
    blocks = (slots, block_size, block_size)
    hbm = lambda shape: pltpu.HBM(shape, F32)
    vmem = lambda shape, dtype=F32: pltpu.VMEM(shape, dtype)
    exchange = functools.partial(lax.all_to_all, split_axis=0, concat_axis=0, tiled=True)
    order = in_hbm(owner_order)

    outgoing, table = pl.pallas_call(
        functools.partial(pack_kernel, out_places),
        out_shape=(vmem(pair), pltpu.SMEM(owner_order.shape, jnp.int32)),
        in_specs=[ANY, ANY],
        out_specs=(VMEM, pl.BlockSpec(memory_space=pltpu.SMEM)),
        scratch_shapes=[
            vmem(grad.shape), pltpu.SMEM((peers * slots,), jnp.int32), DMA((2 * CHUNKS,)), DMA,
        ],
        compiler_params=params(8),
        name="pack",
    )(order, in_hbm(grad))
    arrived = exchange(outgoing, OUT_ORDER)

    shampoo, held, sums = pl.pallas_call(
        functools.partial(mid_kernel, out_places),
        out_shape=(vmem(pair), hbm(pair), jax.ShapeDtypeStruct((ranks, 1, 128), F32)),
        in_specs=[VMEM] * 4,
        out_specs=(VMEM, ANY, VMEM),
        scratch_shapes=[vmem(blocks, BF16), vmem(blocks, BF16), DMA],
        compiler_params=params(16),
        name="mid",
    )(in_vmem(arrived), in_vmem(second), in_vmem(left_root), in_vmem(right_root))
    sums = exchange(sums, (DP + TENSOR)[::-1])

    step = pl.pallas_call(
        functools.partial(step_kernel, back_places),
        out_shape=hbm(pair),
        in_specs=[VMEM] * 3,
        out_specs=ANY,
        scratch_shapes=[vmem(pair), DMA],
        compiler_params=params(8),
        name="step",
    )(sums, in_vmem(shampoo), in_vmem(momentum))
    returned = exchange(step, BACK_ORDER)

    new_left, new_right, new_second, new_momentum = pl.pallas_call(
        functools.partial(rest_kernel, out_places, back_places),
        out_shape=(hbm(blocks),) * 4,
        in_specs=[ANY] * 6,
        out_specs=(ANY,) * 4,
        scratch_shapes=[vmem(pair)] + [vmem(blocks)] * 4 + [vmem(pair)]
        + [vmem(blocks, BF16)] * 2 + [DMA((slots, 6)), DMA],
        compiler_params=params(24),
        cost_estimate=pl.CostEstimate(
            flops=slots * 12 * block_size**3, bytes_accessed=18 * MIB, transcendentals=0
        ),
        name="rest",
    )(
        in_hbm(held), in_hbm(second), in_hbm(left_stat), in_hbm(right_stat),
        in_hbm(momentum), in_hbm(step),
    )

    update = pl.pallas_call(
        functools.partial(unpack_kernel, back_places),
        out_shape=hbm(grad.shape),
        in_specs=[pl.BlockSpec(memory_space=pltpu.SMEM), VMEM],
        out_specs=ANY,
        scratch_shapes=[DMA],
        compiler_params=params(8),
        name="unpack",
    )(table, in_vmem(returned))
    return (new_left, new_right, new_momentum, new_second, update)


def solution(mesh):
    names, sizes = zip(*FINE)
    fine = jax.sharding.Mesh(mesh.devices.reshape(sizes), names)
    owned = P(DP + TENSOR, None, None)
    return jax.shard_map(
        body,
        mesh=fine,
        in_specs=(P(TENSOR, DP), P(DP, None)) + (owned,) * 6,
        out_specs=(owned,) * 4 + (P(TENSOR, DP),),
        check_vma=False,
    )
```

```python
import functools

import jax
import jax.numpy as jnp
import numpy as np
from jax import lax
from jax.experimental import pallas as pl
from jax.experimental.pallas import tpu as pltpu
from jax.sharding import PartitionSpec as P

ANY = pl.BlockSpec(memory_space=pl.ANY)
VMEM = pl.BlockSpec(memory_space=pltpu.VMEM)
DMA = pltpu.SemaphoreType.DMA
MIB = 1 << 20
F32 = jnp.float32
BF16 = jnp.bfloat16
CHUNKS = 4


FINE = (("z", 4), ("yh", 2), ("x", 4), ("yl", 2), ("core", 2))
DP, TENSOR = ("z", "yh"), ("x", "yl", "core")
OUT_ORDER, BACK_ORDER = TENSOR, TENSOR


def places_of(order):
    sizes = dict(FINE)
    places = []
    for at in np.ndindex(*(sizes[axis] for axis in order)):
        where = dict(zip(order, at))
        place = 0
        for axis in TENSOR:
            place = place * sizes[axis] + where[axis]
        places.append(place)
    return places


def in_vmem(x):
    return pltpu.with_memory_space_constraint(x, pltpu.VMEM)


def in_hbm(x):
    return pltpu.with_memory_space_constraint(x, pltpu.HBM)


def params(mib):
    return pltpu.CompilerParams(vmem_limit_bytes=mib * MIB)


def copy(source, target, sem):
    return pltpu.make_async_copy(source, target, sem)


def started(source, target, sem):
    moved = copy(source, target, sem)
    moved.start()
    return moved


def wait_all(ref, sem):
    copy(ref, ref, sem).wait()


def piece_of(ref, block, piece_rows, block_size):
    col_blocks = ref.shape[1] // block_size
    row = pl.multiple_of((block // col_blocks) * piece_rows, piece_rows)
    col = pl.multiple_of((block % col_blocks) * block_size, block_size)
    return ref.at[pl.ds(row, piece_rows), pl.ds(col, block_size)]


def rows_of(peer, piece_rows):
    return slice(peer * piece_rows, (peer + 1) * piece_rows)


def pack_kernel(
    places, order_ref, grad_ref, out_ref, order_here, here_ref, index_ref, sems, order_sem
):
    peers, slots, piece_rows, block_size = out_ref.shape
    table = started(order_ref, order_here, order_sem)
    col_blocks = grad_ref.shape[1] // block_size
    chunk_rows = grad_ref.shape[0] // sems.shape[0]
    loads = []
    for chunk in range(sems.shape[0]):
        rows = pl.ds(chunk * chunk_rows, chunk_rows)
        loads.append(started(grad_ref.at[rows], here_ref.at[rows], sems.at[chunk]))
    table.wait()
    for peer in range(peers):
        for slot in range(slots):
            index_ref[order_here[0, places[peer] * slots + slot]] = peer * slots + slot
    for chunk, load in enumerate(loads):
        load.wait()
        for row in range(chunk * chunk_rows, (chunk + 1) * chunk_rows, piece_rows):
            for column in range(col_blocks):
                at = index_ref[row // piece_rows * col_blocks + column]
                out_ref[at // slots, at % slots] = here_ref[
                    row : row + piece_rows, column * block_size : (column + 1) * block_size
                ]


def unpack_kernel(places, order_ref, moved_ref, out_ref, sem):
    peers, slots, piece_rows, block_size = moved_ref.shape
    for peer in range(peers):
        for slot in range(slots):
            block = order_ref[0, places[peer] * slots + slot]
            started(
                moved_ref.at[peer, slot], piece_of(out_ref, block, piece_rows, block_size), sem
            )
    wait_all(moved_ref, sem)


def sum_rows(x):
    return jnp.sum(x.reshape(-1, 8, x.shape[-1]), axis=0)


def mid_kernel(
    places, arrived_ref, second_ref, left_ref, right_ref, shampoo_ref, held_ref, sums_ref,
    low_ref, applied_ref, sem,
):
    peers, slots, piece_rows, block_size = arrived_ref.shape
    kept = started(arrived_ref, held_ref, sem)
    row_order = sorted(range(peers), key=lambda peer: places[peer])

    adam_sq = jnp.zeros((8, block_size), F32)
    shampoo_sq = jnp.zeros((8, block_size), F32)
    for slot in range(slots):
        for peer in row_order:
            rows = rows_of(places[peer], piece_rows)
            held = arrived_ref[peer, slot]
            low_ref[slot, rows, :] = held.astype(BF16)
            new_second = 0.99 * second_ref[slot, rows, :] + 0.01 * held * held
            adam = held * pl.reciprocal(jnp.sqrt(new_second) + 1e-08)
            adam_sq += sum_rows(adam * adam)
    for slot in range(slots):
        applied_ref[slot] = jnp.dot(
            left_ref[slot], low_ref[slot], preferred_element_type=F32
        ).astype(BF16)
    for slot in range(slots):
        shampoo = jnp.dot(applied_ref[slot], right_ref[slot], preferred_element_type=F32)
        shampoo_ref[:, slot] = shampoo.reshape(peers, piece_rows, block_size)
        shampoo_sq += sum_rows(shampoo * shampoo)
    first = lax.broadcasted_iota(jnp.int32, (1, 128), 1) < 64
    sums = jnp.where(first, jnp.sum(adam_sq), jnp.sum(shampoo_sq))
    sums_ref[...] = jnp.broadcast_to(sums[None], sums_ref.shape)
    kept.wait()


def graft_of(sums_ref):
    root = jnp.sqrt(jnp.sum(sums_ref[...], axis=0))
    return root[0:1, 0:1] / (root[0:1, 64:65] + 1e-06)


def step_kernel(places, sums_ref, shampoo_ref, momentum_ref, step_ref, here_ref, sem):
    peers, slots, piece_rows, block_size = shampoo_ref.shape
    graft = graft_of(sums_ref)
    count = peers // (2 * CHUNKS)
    for peer in range(peers):
        rows = rows_of(places[peer], piece_rows)
        for slot in range(slots):
            scaled = graft * shampoo_ref[places[peer], slot]
            new_momentum = 0.9 * momentum_ref[slot, rows, :] + scaled
            here_ref[peer, slot] = -(0.9 * new_momentum + scaled)
        if peer % count == count - 1:
            part = pl.ds(peer - count + 1, count)
            started(here_ref.at[part], step_ref.at[part], sem)
    wait_all(here_ref, sem)


def rest_kernel(
    out_places, back_places, held_ref, second_ref, left_ref, right_ref, momentum_ref, step_ref,
    new_left_ref, new_right_ref, new_second_ref, new_momentum_ref,
    held_here, second_here, left_here, right_here, momentum_here, step_here, high_ref, low_ref,
    sems, store_sem,
):
    peers, slots, piece_rows, block_size = held_ref.shape

    def load(slot):
        pairs = (
            (left_ref.at[slot], left_here.at[slot]),
            (right_ref.at[slot], right_here.at[slot]),
            (second_ref.at[slot], second_here.at[slot]),
            (momentum_ref.at[slot], momentum_here.at[slot]),
            (step_ref.at[:, slot], step_here.at[:, slot]),
            (held_ref.at[:, slot], held_here.at[:, slot]),
        )[::-1]
        return [started(*pair, sems.at[slot, k]) for k, pair in enumerate(pairs)]

    scale = 0.1 / block_size
    half = block_size // 2
    loads = [load(0)]
    for slot in range(slots):
        loads[slot][0].wait()
        for peer in range(peers):
            rows = rows_of(out_places[peer], piece_rows)
            held = held_here[peer, slot]
            high = held.astype(BF16)
            high_ref[slot, rows, :] = high
            low_ref[slot, rows, :] = (held - high.astype(F32)).astype(BF16)
        for k, (here, ref) in enumerate(
            ((left_here, new_left_ref), (right_here, new_right_ref))
        ):
            product = functools.partial(
                lax.dot_general,
                dimension_numbers=(((1 - k,), (1 - k,)), ((), ())),
                preferred_element_type=F32,
            )
            loads[slot][5 - k].wait()
            for part in range(2):
                cut = slice(part * half, (part + 1) * half)
                at = (slot, cut, slice(None)) if k == 0 else (slot, slice(None), cut)
                gram = (
                    product(high_ref[at], low_ref[slot])
                    + product(low_ref[at], high_ref[slot])
                    + product(high_ref[at], high_ref[slot])
                )
                here[slot, cut, :] = 0.9 * here[slot, cut, :] + scale * gram
            started(here.at[slot], ref.at[slot], store_sem)
        if slot + 1 < slots:
            loads.append(load(slot + 1))
        for pending in loads[slot][1:4]:
            pending.wait()
        for peer in range(peers):
            rows = rows_of(out_places[peer], piece_rows)
            held = held_here[peer, slot]
            second_here[slot, rows, :] = 0.99 * second_here[slot, rows, :] + 0.01 * held * held
            rows = rows_of(back_places[peer], piece_rows)
            momentum_here[slot, rows, :] = (
                0.9 * momentum_here[slot, rows, :] - step_here[peer, slot]
            ) * (1.0 / 1.9)
        started(second_here.at[slot], new_second_ref.at[slot], store_sem)
        started(momentum_here.at[slot], new_momentum_ref.at[slot], store_sem)
    for here in (left_here, right_here, second_here, momentum_here):
        wait_all(here, store_sem)


def body(grad, owner_order, left_stat, right_stat, left_root, right_root, momentum, second):
    slots, block_size = left_stat.shape[0], left_stat.shape[1]
    peers, ranks = lax.axis_size(TENSOR), lax.axis_size(DP + TENSOR)
    out_places, back_places = places_of(OUT_ORDER), places_of(BACK_ORDER)
    piece_rows = block_size // peers
    pair = (peers, slots, piece_rows, block_size)
    blocks = (slots, block_size, block_size)
    hbm = lambda shape: pltpu.HBM(shape, F32)
    vmem = lambda shape, dtype=F32: pltpu.VMEM(shape, dtype)
    exchange = functools.partial(lax.all_to_all, split_axis=0, concat_axis=0, tiled=True)
    order = in_hbm(owner_order)

    outgoing, table = pl.pallas_call(
        functools.partial(pack_kernel, out_places),
        out_shape=(vmem(pair), pltpu.SMEM(owner_order.shape, jnp.int32)),
        in_specs=[ANY, ANY],
        out_specs=(VMEM, pl.BlockSpec(memory_space=pltpu.SMEM)),
        scratch_shapes=[
            vmem(grad.shape), pltpu.SMEM((peers * slots,), jnp.int32), DMA((4 * CHUNKS,)), DMA,
        ],
        compiler_params=params(8),
        name="pack",
    )(order, in_hbm(grad))
    arrived = exchange(outgoing, OUT_ORDER)

    shampoo, held, sums = pl.pallas_call(
        functools.partial(mid_kernel, out_places),
        out_shape=(vmem(pair), hbm(pair), jax.ShapeDtypeStruct((ranks, 1, 128), F32)),
        in_specs=[VMEM] * 4,
        out_specs=(VMEM, ANY, VMEM),
        scratch_shapes=[vmem(blocks, BF16), vmem(blocks, BF16), DMA],
        compiler_params=params(16),
        name="mid",
    )(in_vmem(arrived), in_vmem(second), in_vmem(left_root), in_vmem(right_root))
    sums = exchange(sums, (DP + TENSOR)[::-1])

    step = pl.pallas_call(
        functools.partial(step_kernel, back_places),
        out_shape=hbm(pair),
        in_specs=[VMEM] * 3,
        out_specs=ANY,
        scratch_shapes=[vmem(pair), DMA],
        compiler_params=params(8),
        name="step",
    )(sums, in_vmem(shampoo), in_vmem(momentum))
    returned = exchange(step, BACK_ORDER)

    new_left, new_right, new_second, new_momentum = pl.pallas_call(
        functools.partial(rest_kernel, out_places, back_places),
        out_shape=(hbm(blocks),) * 4,
        in_specs=[ANY] * 6,
        out_specs=(ANY,) * 4,
        scratch_shapes=[vmem(pair)] + [vmem(blocks)] * 4 + [vmem(pair)]
        + [vmem(blocks, BF16)] * 2 + [DMA((slots, 6)), DMA],
        compiler_params=params(24),
        cost_estimate=pl.CostEstimate(
            flops=slots * 12 * block_size**3, bytes_accessed=18 * MIB, transcendentals=0
        ),
        name="rest",
    )(
        in_hbm(held), in_hbm(second), in_hbm(left_stat), in_hbm(right_stat),
        in_hbm(momentum), in_hbm(step),
    )

    update = pl.pallas_call(
        functools.partial(unpack_kernel, back_places),
        out_shape=hbm(grad.shape),
        in_specs=[pl.BlockSpec(memory_space=pltpu.SMEM), VMEM],
        out_specs=ANY,
        scratch_shapes=[DMA],
        compiler_params=params(8),
        name="unpack",
    )(table, in_vmem(returned))
    return (new_left, new_right, new_momentum, new_second, update)


def solution(mesh):
    names, sizes = zip(*FINE)
    fine = jax.sharding.Mesh(mesh.devices.reshape(sizes), names)
    owned = P(DP + TENSOR, None, None)
    return jax.shard_map(
        body,
        mesh=fine,
        in_specs=(P(TENSOR, DP), P(DP, None)) + (owned,) * 6,
        out_specs=(owned,) * 4 + (P(TENSOR, DP),),
        check_vma=False,
    )
```
